32 devices in a mesh: day: 2 (over x), row: 16 (over z, y, core).
Axes of the slice: x: 2, y: 2, z: 4, core: 2. Of those that a mesh axis runs over, the one named last changes fastest.
Arguments:
- spectra: bfloat16 [4096, 2, 2, 4096], P(('day', 'row')), parts along dimension 0, may hold values from -110 to 110
- pair_channels: int32 [64, 128, 2], P('row'), may hold values from 0 to 2047, as said below
- pair_live: int32 [64, 128], P('row'), may hold values from 0 to 1, as said below
Outputs:
- correlations: float32 [128, 128, 512], P(('day', 'row')), parts along dimension 0
The draws below stay inside these ranges and needn't reach their ends.
There are 2 independent parts, one for each index of `day`. The reference program is written for one: setup_inputs(seed, part) draws one part's arguments, and reference() takes and returns one part's arrays. A program takes and returns all parts, laid end to end along the dimension named above; an argument that names none is the same for every part. Nothing has to cross between parts.
Inputs may be any that keep to these rules, and one draw needn't show every extreme that they name: `pair_channels`: pair slots of device i of row are tiles i * 4 to (i + 1) * 4 - 1; their first channels are that device's own channels i * 128 to (i + 1) * 128 - 1, and their second channels lie within 128 channels of the first; distances of exactly 128 occur on both sides. `pair_live`: in each device's pair slots (tile by tile, pair by pair) the live slots come first and the padding after; every device has 128 live slots or more, and one device's slots are all live.
All inputs are finite; a program needn't handle non-finite values.
Results may differ from the reference program's by a relative error of at most 0.003.
Values may be sent and summed in bfloat16 or wider, within the bound.
No kernel may reach another device: no remote copies, remote signals or barrier semaphores. Data moves between devices by JAX's collectives and lax.ppermute only.
A program may use at most 192 MiB of HBM per device.

```python
import math
import jax
import jax.numpy as jnp
from jax import lax

CH_DEV = 128
TILE_SLOTS = 4
WIN = 2
FREQ = 4096
BAND = 64
LAGS = 512
BLOCK = 128
HALO = 128
CHANNELS = 2048
TILES = 64


def pair_tables(key):
    device_count = TILES // TILE_SLOTS
    per_device = TILE_SLOTS * BLOCK
    base_key = jax.random.fold_in(key, 7)
    first_key, offset_key, count_key, full_key = jax.random.split(base_key, 4)
    own_offset = jax.random.randint(first_key, (device_count, per_device), 0, CH_DEV)
    reach_chan = jax.random.randint(offset_key, (device_count, per_device), -HALO, HALO + 1)
    own_offset = own_offset.at[:, 0].set(0).at[:, 1].set(CH_DEV - 1)
    reach_chan = reach_chan.at[:, 0].set(-HALO).at[:, 1].set(HALO)
    device_rows = jnp.arange(device_count, dtype=jnp.int32)[:, None]
    first_chan = device_rows * CH_DEV + own_offset
    second_chan = first_chan + reach_chan
    outside = (second_chan < 0) | (second_chan >= CHANNELS)
    second_chan = jnp.where(outside, first_chan - reach_chan, second_chan)
    live_count = jax.random.randint(count_key, (device_count,), BLOCK, per_device * 3 // 4 + 1)
    full_device = jax.random.randint(full_key, (), 0, device_count)
    live_count = jnp.where(jnp.arange(device_count) == full_device, per_device, live_count)
    live_mask = (jnp.arange(per_device)[None, :] < live_count[:, None]).astype(jnp.int32)
    pair_table = jnp.stack([first_chan, second_chan], axis=-1).reshape(TILES, BLOCK, 2)
    return (pair_table.astype(jnp.int32), live_mask.reshape(TILES, BLOCK))


def draw_pair_channels(key, part):
    return pair_tables(key)[0]


def draw_pair_live(key, part):
    return pair_tables(key)[1]


def draw_spectra(key, part):
    key_list = jax.random.split(jax.random.fold_in(key, 11), 5)
    position = jnp.arange(CHANNELS, dtype=jnp.float32) / (CHANNELS - 1)
    coupling = (1.0 + 2.0 * position) * jnp.exp(jax.random.uniform(key_list[0], (CHANNELS,), minval=-0.5, maxval=0.5))
    bin_scale = jnp.exp(jax.random.uniform(key_list[1], (FREQ,), minval=math.log(0.3), maxval=math.log(3.0)))
    shape_all = (CHANNELS, WIN, 2, FREQ)
    row_scale = jnp.exp(jax.random.uniform(key_list[2], (CHANNELS,), minval=math.log(0.3), maxval=math.log(3.0)))
    common = jnp.clip(jax.random.normal(key_list[3], (WIN, 2, FREQ)), -5.0, 5.0)
    noise_part = jnp.clip(jax.random.normal(key_list[4], shape_all), -5.0, 5.0)
    values = coupling[:, None, None, None] * common[None] + 0.6 * row_scale[:, None, None, None] * noise_part
    return (values * bin_scale).astype(jnp.bfloat16)


def setup_inputs(seed: int = 0, part: int = 0) -> dict:
    key_of = jax.random.split(jax.random.key(seed), 4)
    part_keys = jax.random.split(jax.random.fold_in(key_of[3], part), 4)
    spectra = draw_spectra(jax.random.fold_in(jax.random.fold_in(key_of[3], part), 71), part)
    pair_channels = draw_pair_channels(jax.random.fold_in(key_of[3], 71), part)
    pair_live = draw_pair_live(jax.random.fold_in(key_of[3], 71), part)
    return {"spectra": spectra, "pair_channels": pair_channels, "pair_live": pair_live}


def build_table(bin_total, lag_total):
    bin_index = jnp.arange(bin_total, dtype=jnp.int32)[:, None]
    shifts = jnp.arange(lag_total, dtype=jnp.int32)[None, :] - lag_total // 2
    phase_int = jnp.mod(bin_index * shifts, 2 * bin_total)
    angle_rad = phase_int.astype(jnp.float32) * (math.pi / bin_total)
    return jnp.concatenate([jnp.cos(angle_rad), -jnp.sin(angle_rad)], axis=0).astype(jnp.bfloat16)

def whiten(raw_rows, common):
    removed = raw_rows.astype(jnp.float32) - common[None]
    magnitude = jnp.sqrt(removed[:, :, 0] ** 2 + removed[:, :, 1] ** 2)
    row_count, window_count, bin_count = magnitude.shape
    banded = magnitude.reshape(row_count, window_count, bin_count // BAND, BAND)
    band_level = lax.optimization_barrier(jnp.mean(banded, axis=3, keepdims=True)) + 1e-06
    scaled = removed.reshape(row_count, window_count, 2, bin_count // BAND, BAND) / band_level[:, :, None]
    return scaled.reshape(raw_rows.shape).astype(jnp.bfloat16)

def cross_rows(first_rows, second_rows):
    first_f32 = first_rows.astype(jnp.float32)
    second_f32 = second_rows.astype(jnp.float32)
    real_part = lax.optimization_barrier(jnp.sum(first_f32[:, :, 0] * second_f32[:, :, 0] + first_f32[:, :, 1] * second_f32[:, :, 1], axis=1))
    imag_part = lax.optimization_barrier(jnp.sum(first_f32[:, :, 1] * second_f32[:, :, 0] - first_f32[:, :, 0] * second_f32[:, :, 1], axis=1))
    return jnp.concatenate([real_part, imag_part], axis=1).astype(jnp.bfloat16)

def reference(spectra, pair_channels, pair_live):
    common = lax.optimization_barrier(jnp.sum(spectra, axis=0, dtype=jnp.float32)) / CHANNELS
    whitened = whiten(spectra, common)
    lag_matrix = build_table(FREQ, LAGS)
    norm_factor = 1.0 / math.sqrt(FREQ * WIN)

    def one_tile(operands):
        tile_pairs, tile_live = operands
        products = cross_rows(whitened[tile_pairs[:, 0]], whitened[tile_pairs[:, 1]])
        summed = jnp.dot(products, lag_matrix, preferred_element_type=jnp.float32)
        return summed * norm_factor * tile_live.astype(jnp.float32)[:, None]
    return lax.map(one_tile, (pair_channels, pair_live))
```

```python
import functools
import math

import jax
import jax.numpy as jnp
import numpy as np
from jax import lax
from jax.experimental import pallas as pl
from jax.experimental.pallas import tpu as pltpu
from jax.sharding import PartitionSpec as P

BAND = 64
LAGS = 512
STEP = 512
GROUP = 256
BLOCK1 = 256
BLOCK2 = 128
SLOW_CHUNKS = 2
VMEM_BYTES = 48 * 1024 * 1024
F32 = jnp.float32
BF16 = jnp.bfloat16


def lag_table(bins, lags):
    shifts = np.arange(lags, dtype=np.int64)[None, :] - lags // 2
    phase = np.mod(np.arange(bins, dtype=np.int64)[:, None] * shifts, 2 * bins)
    angle = (phase.astype(np.float32) * np.float32(math.pi / bins)).astype(np.float64)
    both = np.stack([np.cos(angle), -np.sin(angle)]).astype(np.float32)
    return both.astype(jnp.bfloat16)


def band_mean():
    rows = np.arange(GROUP)[:, None] // BAND
    cols = np.arange(GROUP)[None, :] // BAND
    return np.where(rows == cols, 1.0 / BAND, 0.0).astype(jnp.bfloat16)


def dot(a, b):
    return jnp.dot(a, b, preferred_element_type=F32)


def whiten_into(w_ref, row0, raws, commons, mean_ref):
    windows = len(raws)
    rows, bins = raws[0][0].shape
    for w in range(windows):
        for g in range(bins // GROUP):
            cols = pl.ds(g * GROUP, GROUP)
            re = raws[w][0][:, cols].astype(F32) - commons[w][0][:, cols]
            im = raws[w][1][:, cols].astype(F32) - commons[w][1][:, cols]
            magnitude = jnp.sqrt(re * re + im * im)
            high = magnitude.astype(BF16)
            low = (magnitude - high.astype(F32)).astype(BF16)
            level = dot(high, mean_ref[...]) + dot(low, mean_ref[...]) + 1e-06
            scale = 1.0 / level
            target = pl.ds(row0, rows)
            w_ref[target, pl.ds((2 * w) * bins + g * GROUP, GROUP)] = (re * scale).astype(BF16)
            w_ref[target, pl.ds((2 * w + 1) * bins + g * GROUP, GROUP)] = (im * scale).astype(BF16)


def one_hot(index_ref, hot_ref):
    slots, rows = hot_ref.shape
    lane = lax.broadcasted_iota(jnp.int32, (slots, rows), 1)
    hot_ref[...] = jnp.where(index_ref[...] == lane, 1.0, 0.0).astype(BF16)


def correlate_block(hot_a, hot_b, w_ref, table_ref, windows, start, size):
    bins = w_ref.shape[1] // (2 * windows)
    rows = pl.ds(start, size)
    a = dot(hot_a[rows, :], w_ref[...])
    b = dot(hot_b[rows, :], w_ref[...])
    real = imag = None
    for w in range(windows):
        ar, ai = (a[:, (2 * w + r) * bins : (2 * w + r + 1) * bins] for r in range(2))
        br, bi = (b[:, (2 * w + r) * bins : (2 * w + r + 1) * bins] for r in range(2))
        re = ar * br + ai * bi
        im = ai * br - ar * bi
        real = re if real is None else real + re
        imag = im if imag is None else imag + im
    return dot(real.astype(BF16), table_ref[0]) + dot(imag.astype(BF16), table_ref[1])


def near_kernel(windows, live_ref, *refs):
    parts = 2 * windows
    own = refs[:parts]
    other = refs[parts : 2 * parts]
    common = refs[2 * parts : 3 * parts]
    table_ref, mean_ref, ia_ref, ib_ref = refs[3 * parts : 3 * parts + 4]
    acc_ref = refs[3 * parts + 4]
    white = refs[3 * parts + 5 : 4 * parts + 5]
    w_ref, hot_a, hot_b = refs[4 * parts + 5 :]
    step = pl.program_id(0)

    @pl.when(step == 0)
    def _():
        acc_ref[...] = jnp.zeros_like(acc_ref)
        one_hot(ia_ref, hot_a)
        one_hot(ib_ref, hot_b)

    pairs = [common[2 * w : 2 * w + 2] for w in range(windows)]
    rows = own[0].shape[0]
    bins = own[0].shape[1]
    whiten_into(w_ref, 0, [own[2 * w : 2 * w + 2] for w in range(windows)], pairs, mean_ref)
    whiten_into(w_ref, rows, [other[2 * w : 2 * w + 2] for w in range(windows)], pairs, mean_ref)
    for part in range(parts):
        white[part][...] = w_ref[pl.ds(0, rows), pl.ds(part * bins, bins)]
    for block in range(hot_a.shape[0] // BLOCK1):

        @pl.when(block * BLOCK1 < live_ref[0])
        def _():
            acc_ref[pl.ds(block * BLOCK1, BLOCK1), :] += correlate_block(
                hot_a, hot_b, w_ref, table_ref, windows, block * BLOCK1, BLOCK1
            )


def far_kernel(windows, first, info_ref, *refs):
    parts = 2 * windows
    white = refs[:parts]
    other = refs[parts : 2 * parts]
    common = refs[2 * parts : 3 * parts]
    table_ref, mean_ref, ia_ref, ib_ref = refs[3 * parts : 3 * parts + 4]
    rest = refs[3 * parts + 4 :]
    if first:
        acc_ref, w_ref, hot_a, hot_b = rest
    else:
        before_ref, acc_ref, w_ref, hot_a, hot_b = rest
    step = pl.program_id(0)

    @pl.when(step == 0)
    def _():
        acc_ref[...] = jnp.zeros_like(acc_ref) if first else before_ref[...]
        one_hot(ia_ref, hot_a)
        one_hot(ib_ref, hot_b)

    pairs = [common[2 * w : 2 * w + 2] for w in range(windows)]
    rows, bins = other[0].shape
    for part in range(parts):
        w_ref[pl.ds(0, rows), pl.ds(part * bins, bins)] = white[part][...]
    whiten_into(w_ref, rows, [other[2 * w : 2 * w + 2] for w in range(windows)], pairs, mean_ref)
    slots = hot_a.shape[0]
    for block in range(slots // BLOCK2):
        inside = block * BLOCK2 % (slots // 2)

        @pl.when(inside < info_ref[1 + block * BLOCK2 // (slots // 2)])
        def _():
            acc_ref[pl.ds(block * BLOCK2, BLOCK2), :] += correlate_block(
                hot_a, hot_b, w_ref, table_ref, windows, block * BLOCK2, BLOCK2
            )


def sum_kernel(x_ref, o_ref):
    ones = jnp.ones((8, x_ref.shape[0]), BF16)
    o_ref[...] = dot(ones, x_ref[...])[0:1]


def merge_kernel(scale, near_ref, far_ref, back_ref, position_ref, live_ref, o_ref):
    slots = near_ref.shape[0]
    lane = lax.broadcasted_iota(jnp.int32, (slots, slots), 1)
    spread = jnp.where(position_ref[...] == lane, 1.0, 0.0).astype(BF16)
    far = far_ref[...]
    high = far.astype(BF16)
    low = (far - high.astype(F32)).astype(BF16)
    total = near_ref[...] + (dot(spread, high) + dot(spread, low) + dot(spread, back_ref[...]))
    o_ref[...] = total * scale * live_ref[...]


def params(cost_flops, cost_bytes):
    return dict(
        compiler_params=pltpu.CompilerParams(vmem_limit_bytes=VMEM_BYTES),
        cost_estimate=pl.CostEstimate(
            flops=cost_flops, bytes_accessed=cost_bytes, transcendentals=0
        ),
    )


def compact(crossing, row_a, row_b):
    slots = crossing.shape[0]
    order = jnp.arange(slots, dtype=jnp.int32)
    flag = crossing.astype(jnp.int32)
    ahead = jnp.sum(jnp.where(order[None, :] < order[:, None], flag[None, :], 0), axis=1)
    place = jnp.where(crossing, ahead, -1)
    match = place[None, :] == order[:, None]
    a = jnp.sum(jnp.where(match, row_a[None, :] + 1, 0), axis=1) - 1
    b = jnp.sum(jnp.where(match, row_b[None, :] + 1, 0), axis=1) - 1
    return a, b, place, jnp.sum(flag)


def body(spectra, pair_channels, pair_live):
    rows, windows, _, bins = spectra.shape
    parts = 2 * windows
    count = lax.axis_size("row")
    me = lax.axis_index("row")
    odd = me % 2
    first_row = me * rows
    half = bins // 2
    fast = [(i, i ^ 1) for i in range(count)]
    slow = [(i, i + 1) for i in range(1, count - 1, 2)]
    slow = slow + [(b, a) for a, b in slow]

    chunk = half // SLOW_CHUNKS
    send_start = (1 - odd) * half
    sent = [
        lax.dynamic_slice_in_dim(spectra, send_start + c * chunk, chunk, axis=3).reshape(
            rows, parts * chunk
        )
        for c in range(SLOW_CHUNKS)
    ]
    far_rows = [lax.ppermute(part, "row", slow) for part in sent]

    flat = spectra.reshape(rows, parts * bins)
    partner_rows = lax.ppermute(flat, "row", fast)

    wide = parts * bins // 8
    total = pl.pallas_call(
        sum_kernel,
        grid=(8,),
        in_specs=[pl.BlockSpec((rows, wide), lambda j: (0, j))],
        out_specs=pl.BlockSpec((1, wide), lambda j: (0, j)),
        out_shape=jax.ShapeDtypeStruct((1, parts * bins), F32),
        name="local_sum",
        **params(2 * rows * parts * bins, 2 * rows * parts * bins),
    )(flat)
    if count & (count - 1):
        total = lax.psum(total, "row")
    else:
        jump = 1
        while jump < count:
            total = total + lax.ppermute(total, "row", [(i, i ^ jump) for i in range(count)])
            jump *= 2
    common = total / (rows * count)

    slots = pair_channels.shape[0] * pair_channels.shape[1]
    pairs = pair_channels.reshape(slots, 2)
    live = pair_live.reshape(slots)
    listed = jnp.concatenate([pairs, live[:, None]], axis=1)
    far_listed = lax.ppermute(listed, "row", slow)
    order = jnp.arange(slots, dtype=jnp.int32)
    live_end = jnp.max(jnp.where(live != 0, order + 1, 0))
    near_shift = jnp.where(odd == 1, -rows, rows)
    far_shift = -near_shift
    row_a = pairs[:, 0] - first_row
    offset = pairs[:, 1] - first_row
    in_own = (offset >= 0) & (offset < rows)
    in_near = (offset >= near_shift) & (offset < near_shift + rows)
    in_far = (offset >= far_shift) & (offset < far_shift + rows)
    near_b = jnp.where(in_own, offset, jnp.where(in_near, offset - near_shift + rows, -1))
    own_a, own_b, place, own_count = compact(
        in_far & (live != 0), row_a, offset - far_shift + rows
    )
    far_a = far_listed[:, 0] - (first_row + far_shift) + rows
    far_b = far_listed[:, 1] - first_row
    their_a, their_b, _, their_count = compact(
        (far_b >= 0) & (far_b < rows) & (far_listed[:, 2] != 0), far_a, far_b
    )
    cross_a = jnp.concatenate([own_a, their_a])[:, None]
    cross_b = jnp.concatenate([own_b, their_b])[:, None]

    table = jnp.asarray(lag_table(bins, LAGS))
    mean = jnp.asarray(band_mean())
    steps = bins // STEP

    def whole(shape):
        return pl.BlockSpec(shape, lambda *_: (0,) * len(shape))

    near_acc, *white = pl.pallas_call(
        functools.partial(near_kernel, windows),
        grid_spec=pltpu.PrefetchScalarGridSpec(
            num_scalar_prefetch=1,
            grid=(steps,),
            in_specs=[
                pl.BlockSpec((n, STEP), functools.partial(lambda p, j, s: (0, p * steps + j), p))
                for n in (rows, rows, 1)
                for p in range(parts)
            ]
            + [
                pl.BlockSpec((2, STEP, LAGS), lambda j, s: (0, j, 0)),
                whole((GROUP, GROUP)),
                whole((slots, 1)),
                whole((slots, 1)),
            ],
            out_specs=[whole((slots, LAGS))]
            + [pl.BlockSpec((rows, STEP), lambda j, s: (0, j)) for _ in range(parts)],
            scratch_shapes=[
                pltpu.VMEM((2 * rows, parts * STEP), BF16),
                pltpu.VMEM((slots, 2 * rows), BF16),
                pltpu.VMEM((slots, 2 * rows), BF16),
            ],
        ),
        out_shape=[jax.ShapeDtypeStruct((slots, LAGS), F32)]
        + [jax.ShapeDtypeStruct((rows, bins), BF16) for _ in range(parts)],
        name="near_pairs",
        **params(20 * 10**9, 20 * 10**6),
    )(
        live_end[None],
        *[flat] * parts,
        *[partner_rows] * parts,
        *[common] * parts,
        table,
        mean,
        row_a[:, None],
        near_b[:, None],
    )

    chunk_steps = chunk // STEP
    info = jnp.stack([odd * (half // STEP), own_count, their_count])
    far_acc = None
    for c in range(SLOW_CHUNKS):
        own_map = functools.partial(lambda c, j, s: (0, s[0] + c * chunk_steps + j), c)
        specs = (
            [pl.BlockSpec((rows, STEP), own_map) for _ in range(parts)]
            + [
                pl.BlockSpec(
                    (rows, STEP), functools.partial(lambda p, j, s: (0, p * chunk_steps + j), p)
                )
                for p in range(parts)
            ]
            + [
                pl.BlockSpec(
                    (1, STEP),
                    functools.partial(
                        lambda c, p, j, s: (0, p * steps + s[0] + c * chunk_steps + j), c, p
                    ),
                )
                for p in range(parts)
            ]
            + [
                pl.BlockSpec(
                    (2, STEP, LAGS),
                    functools.partial(lambda c, j, s: (0, s[0] + c * chunk_steps + j, 0), c),
                ),
                whole((GROUP, GROUP)),
                whole((2 * slots, 1)),
                whole((2 * slots, 1)),
            ]
        )
        operands = [
            info,
            *white,
            *[far_rows[c]] * parts,
            *[common] * parts,
            table,
            mean,
            cross_a,
            cross_b,
        ]
        if c:
            specs.append(whole((2 * slots, LAGS)))
            operands.append(far_acc)
        far_acc = pl.pallas_call(
            functools.partial(far_kernel, windows, c == 0),
            grid_spec=pltpu.PrefetchScalarGridSpec(
                num_scalar_prefetch=1,
                grid=(chunk_steps,),
                in_specs=specs,
                out_specs=whole((2 * slots, LAGS)),
                scratch_shapes=[
                    pltpu.VMEM((2 * rows, parts * STEP), BF16),
                    pltpu.VMEM((2 * slots, 2 * rows), BF16),
                    pltpu.VMEM((2 * slots, 2 * rows), BF16),
                ],
            ),
            out_shape=jax.ShapeDtypeStruct((2 * slots, LAGS), F32),
            name="far_pairs",
            **params(10 * 10**9 // SLOW_CHUNKS, 10 * 10**6 // SLOW_CHUNKS),
        )(*operands)

    back = lax.ppermute(far_acc[slots:].astype(BF16), "row", slow)
    result = pl.pallas_call(
        functools.partial(merge_kernel, 1.0 / math.sqrt(bins * windows)),
        grid=(1,),
        in_specs=[
            whole((slots, LAGS)),
            whole((slots, LAGS)),
            whole((slots, LAGS)),
            whole((slots, 1)),
            whole((slots, 1)),
        ],
        out_specs=whole((slots, LAGS)),
        out_shape=jax.ShapeDtypeStruct((slots, LAGS), F32),
        name="merge",
        **params(10**9, 4 * 10**6),
    )(near_acc, far_acc, back, place[:, None], live.astype(F32)[:, None])
    return result.reshape(pair_live.shape + (LAGS,))


def solution(mesh):
    placed = (P(("day", "row"), None, None, None), P("row", None, None), P("row", None))
    return jax.shard_map(
        body, mesh=mesh, in_specs=placed, out_specs=P(("day", "row"), None, None), check_vma=False
    )
```

```python
import functools
import math

import jax
import jax.numpy as jnp
import numpy as np
from jax import lax
from jax.experimental import pallas as pl
from jax.experimental.pallas import tpu as pltpu
from jax.sharding import PartitionSpec as P

BAND = 64
LAGS = 512
GROUP = 256
NEAR_GROUPS = 4
FAR_BLOCK = 256
BACK_ROWS = 160
ROW_BLOCK = 16
TINY = 1e-37
VMEM_BYTES = 56 * 1024 * 1024
F32 = jnp.float32
BF16 = jnp.bfloat16


def lag_table(bins, lags):
    shifts = np.arange(lags, dtype=np.int64)[None, :] - lags // 2
    phase = np.mod(np.arange(bins, dtype=np.int64)[:, None] * shifts, 2 * bins)
    angle = (phase.astype(np.float32) * np.float32(math.pi / bins)).astype(np.float64)
    both = np.stack([np.cos(angle), -np.sin(angle)]).astype(np.float32)
    return both.astype(jnp.bfloat16)


def band_mean():
    rows = np.arange(GROUP)[:, None] // BAND
    cols = np.arange(GROUP)[None, :] // BAND
    return np.where(rows == cols, 1.0 / BAND, 0.0).astype(jnp.bfloat16)


def dot(a, b):
    return jnp.dot(a, b, preferred_element_type=F32)


def whiten_into(w_ref, row0, raws, common_ref, mean_ref, start):
    rows = raws[0].shape[0]
    target = pl.ds(row0, rows)
    cols = pl.ds(start, GROUP)
    for w in range(len(raws) // 2):
        re = raws[2 * w][:, cols].astype(F32) - common_ref[w, 0:1, cols]
        im = raws[2 * w + 1][:, cols].astype(F32) - common_ref[w, 1:2, cols]
        power = re * re + im * im
        magnitude = (power * lax.rsqrt(jnp.maximum(power, TINY))).astype(BF16)
        scale = 1.0 / (dot(magnitude, mean_ref[...]) + 1e-06)
        w_ref[target, pl.ds(2 * w * GROUP, GROUP)] = (re * scale).astype(BF16)
        w_ref[target, pl.ds((2 * w + 1) * GROUP, GROUP)] = (im * scale).astype(BF16)


def columns_of(rows_of_tiles):
    lanes = rows_of_tiles.shape[1]
    padded = rows_of_tiles.astype(F32)
    if missing := -padded.shape[0] % 8:
        padded = jnp.concatenate([padded, jnp.zeros((missing, lanes), F32)], axis=0)
    square = (lanes, lanes)
    same = lax.broadcasted_iota(jnp.int32, square, 0) == lax.broadcasted_iota(jnp.int32, square, 1)
    unit = jnp.where(same, 1.0, 0.0).astype(BF16)
    return lax.dot_general(
        unit, padded.astype(BF16), (((1,), (1,)), ((), ())), preferred_element_type=F32
    )


def hot_rows(column, width):
    lane = lax.broadcasted_iota(jnp.int32, (column.shape[0], width), 1).astype(F32)
    return jnp.where(column == lane, 1.0, 0.0).astype(BF16)


def fill_hot(values, hot_ref):
    tiles, lanes = values.shape
    columns = columns_of(values)
    for tile in range(tiles):
        hot_ref[pl.ds(tile * lanes, lanes), :] = hot_rows(
            columns[:, tile : tile + 1], hot_ref.shape[1]
        )


def correlate_rows(hot_a, hot_b, w_ref, table_ref, start):
    both = dot(jnp.concatenate([hot_a, hot_b], axis=0), w_ref[...])
    a, b = both[: hot_a.shape[0]], both[hot_a.shape[0] :]
    real = imag = None
    for w in range(w_ref.shape[1] // (2 * GROUP)):
        ar, ai, br, bi = (
            x[:, (2 * w + r) * GROUP : (2 * w + r + 1) * GROUP] for x in (a, b) for r in range(2)
        )
        re = ar * br + ai * bi
        im = ai * br - ar * bi
        real = re if real is None else real + re
        imag = im if imag is None else imag + im
    rows = pl.ds(start, GROUP)
    return dot(real.astype(BF16), table_ref[0, rows, :]) + dot(
        imag.astype(BF16), table_ref[1, rows, :]
    )


def near_kernel(parts, first, info_ref, *refs):
    refs = list(refs)

    def take(number):
        taken = refs[:number]
        del refs[:number]
        return taken

    own, other = take(parts), take(parts)
    common_ref, table_ref, mean_ref, first_ref, offset_ref, live_ref, before_ref = take(7)
    (acc_ref,) = take(1)
    white = take(parts) if first else []
    hot_a, hot_b, *held = refs
    rows = own[0].shape[0]

    @pl.when(pl.program_id(0) == 0)
    def _():
        acc_ref[...] = jnp.zeros_like(acc_ref) if first else before_ref[...]
        shift = info_ref[0]
        offset = offset_ref[...]
        live = live_ref[...] != 0
        inside = (offset >= 0) & (offset < rows)
        beside = (offset >= shift) & (offset < shift + rows)
        place = jnp.where(inside, offset, jnp.where(beside, offset - shift + rows, -1))
        fill_hot(jnp.where(live, first_ref[...], -1), hot_a)
        fill_hot(jnp.where(live, place, -1), hot_b)

    def prepare(group):
        start = group * GROUP
        w_ref = held[group]
        whiten_into(w_ref, 0, own, common_ref, mean_ref, start)
        whiten_into(w_ref, rows, other, common_ref, mean_ref, start)
        for part in range(len(white)):
            white[part][:, pl.ds(start, GROUP)] = w_ref[
                pl.ds(0, rows), pl.ds(part * GROUP, GROUP)
            ]

    def run(block):
        slots = pl.ds(0, block)
        prepare(0)
        for group in range(len(held)):
            if group + 1 < len(held):
                prepare(group + 1)
            acc_ref[slots, :] += correlate_rows(
                hot_a[slots, :], hot_b[slots, :], held[group], table_ref, group * GROUP
            )

    total = hot_a.shape[0]
    pl.when(info_ref[1] <= total // 2)(lambda: run(total // 2))
    pl.when(info_ref[1] > total // 2)(lambda: run(total))


def plan_kernel(info_ref, first_ref, offset_ref, live_ref, code_ref, _, hot_a, hot_b, spread, back, rest, count_ref):
    tiles, lanes = first_ref.shape
    rows = hot_a.shape[1] // 2
    shift = info_ref[0]
    code = code_ref[...].astype(F32).astype(jnp.int32)
    far_a = code[0:tiles]
    far_b = far_a + code[tiles : 2 * tiles] + shift
    theirs = (far_b >= 0) & (far_b < rows) & (code[2 * tiles : 3 * tiles] != 0)
    offset = offset_ref[...]
    owns = (offset >= shift) & (offset < shift + rows) & (live_ref[...] != 0)
    cross = jnp.concatenate([theirs.astype(F32), owns.astype(F32)], axis=0)
    values_a = jnp.concatenate([far_a + rows, first_ref[...]], axis=0)
    values_b = jnp.concatenate([far_b, offset - shift + rows], axis=0)
    square = (lanes, lanes)
    row = lax.broadcasted_iota(jnp.int32, square, 0)
    col = lax.broadcasted_iota(jnp.int32, square, 1)
    ahead = jnp.where(row < col, 1.0, 0.0).astype(BF16)
    within = dot(cross.astype(BF16), ahead)
    sums = jnp.sum(cross, axis=1, keepdims=True)
    slots = hot_a.shape[0]
    packed = lax.broadcasted_iota(jnp.int32, (slots, lanes), 0).astype(F32)
    lane_rows = lax.broadcasted_iota(jnp.int32, (2 * rows, lanes), 0)
    base = jnp.zeros((1, 1), F32)
    total_a = jnp.zeros(hot_a.shape, F32)
    total_b = jnp.zeros(hot_b.shape, F32)
    bases = []
    for tile in range(2 * tiles):
        bases.append(base)
        place = jnp.where(cross[tile : tile + 1] > 0, within[tile : tile + 1] + base, -1.0)
        select = jnp.where(packed == place, 1.0, 0.0).astype(BF16)
        for values, which in ((values_a, 0), (values_b, 1)):
            ones = jnp.where(lane_rows == values[tile : tile + 1], 1.0, 0.0).astype(BF16)
            part = lax.dot_general(
                select, ones, (((1,), (1,)), ((), ())), preferred_element_type=F32
            )
            if which:
                total_b = total_b + part
            else:
                total_a = total_a + part
        base = base + sums[tile : tile + 1]
    hot_a[...] = total_a.astype(BF16)
    hot_b[...] = total_b.astype(BF16)
    within_columns = columns_of(within)
    cross_columns = columns_of(cross)
    for tile in range(tiles):
        mine = tiles + tile
        live_column = cross_columns[:, mine : mine + 1] > 0
        column = within_columns[:, mine : mine + 1] + bases[mine]
        target = pl.ds(tile * lanes, lanes)
        spread[target, :] = hot_rows(jnp.where(live_column, column, -1.0), spread.shape[1])
        column = jnp.where(live_column, column - bases[tiles], -1.0)
        back[target, :] = hot_rows(column, back.shape[1])
        rest[target, :] = hot_rows(column - back.shape[1], rest.shape[1])
    count_ref[0] = jnp.sum(cross).astype(jnp.int32)


def far_kernel(parts, pieces, first, info_ref, count_ref, *refs):
    refs = list(refs)

    def take(number):
        taken = refs[:number]
        del refs[:number]
        return taken

    white = [take(parts) for _ in range(pieces)]
    other = [take(parts) for _ in range(pieces)]
    common = take(pieces)
    table = take(pieces)
    mean_ref, hot_a, hot_b = take(3)
    (before_ref,) = take(1)
    acc_ref = take(1)[0]
    sent_ref, rest_ref = (None, None) if first else take(2)
    work_ref, load_sem, store_sem = take(3)
    held = refs
    rows, piece = other[0][0].shape
    blocks = (count_ref[0] + FAR_BLOCK - 1) // FAR_BLOCK

    def span(block):
        return pl.ds(pl.multiple_of(block * FAR_BLOCK, FAR_BLOCK), FAR_BLOCK)

    def load(block):
        return pltpu.make_async_copy(
            before_ref.at[span(block), :], work_ref.at[span(block), :], load_sem.at[block]
        )

    def store(block):
        return pltpu.make_async_copy(
            work_ref.at[span(block), :], acc_ref.at[span(block), :], store_sem.at[block]
        )

    if not first:
        lax.fori_loop(0, blocks, lambda block, _: load(block).start(), None)
    each = piece // GROUP
    for number, w_ref in enumerate(held):
        at, start = number // each, number % each * GROUP
        for part in range(parts):
            w_ref[pl.ds(0, rows), pl.ds(part * GROUP, GROUP)] = white[at][part][
                :, pl.ds(start, GROUP)
            ]
        whiten_into(w_ref, rows, other[at], common[at], mean_ref, start)

    def one_block(block, _):
        target = span(block)
        gained = None
        for number, w_ref in enumerate(held):
            at, start = number // each, number % each * GROUP
            part = correlate_rows(hot_a[target, :], hot_b[target, :], w_ref, table[at], start)
            gained = part if gained is None else gained + part
        if first:
            work_ref[target, :] = gained
        else:
            load(block).wait()
            work_ref[target, :] += gained
        store(block).start()

    lax.fori_loop(0, blocks, one_block, None)
    if not first:
        sent = sent_ref.shape[0]
        used = lax.broadcasted_iota(jnp.int32, (sent + rest_ref.shape[0], 1), 0)
        used = used < blocks * FAR_BLOCK
        for ref, at in ((sent_ref, 0), (rest_ref, sent)):
            ours = slice(at, at + ref.shape[0])
            ref[...] = jnp.where(used[ours], work_ref[ours, :], 0.0).astype(BF16)
    lax.fori_loop(0, blocks, lambda block, _: store(block).wait(), None)


def prepare_kernel(width, counts, info_ref, x_ref, pairs_ref, live_ref, flat_ref, total_ref, *sent):
    bins = x_ref.shape[3]
    parts = flat_ref.shape[1] // bins
    flat_ref[...] = x_ref[...].reshape(flat_ref.shape)
    total = x_ref[0].astype(F32)
    for row in range(1, x_ref.shape[0]):
        total = total + x_ref[row].astype(F32)

    @pl.when(pl.program_id(0) == 0)
    def _():
        total_ref[:, :, pl.ds(0, bins)] = total
        second = pairs_ref[...][:, 1, :] - info_ref[1]
        crossing = (second >= 0) & (second < info_ref[2]) & (live_ref[...] != 0)
        number = jnp.sum(jnp.where(crossing, 1.0, 0.0))
        flag = jnp.where(number > BACK_ROWS, 1.0, 0.0)
        lanes = total_ref.shape[2] - bins
        total_ref[:, :, pl.ds(bins, lanes)] = jnp.full(total_ref.shape[:2] + (lanes,), flag, F32)

    @pl.when(pl.program_id(0) > 0)
    def _():
        total_ref[:, :, pl.ds(0, bins)] += total

    done = 0
    for pieces, ref in zip(counts, sent):
        for part in range(parts):
            start = part * bins + done * width + info_ref[0]
            ref[:, pl.ds(part * pieces * width, pieces * width)] = flat_ref[
                :, pl.ds(pl.multiple_of(start, width), pieces * width)
            ]
        done += pieces


def gather_kernel(scale, count_ref, near_ref, spread_ref, far_ref, o_ref, held, sem):
    blocks = (count_ref[0] + FAR_BLOCK - 1) // FAR_BLOCK

    def load(block):
        rows = pl.ds(pl.multiple_of(block * FAR_BLOCK, FAR_BLOCK), FAR_BLOCK)
        return pltpu.make_async_copy(far_ref.at[rows, :], held.at[rows, :], sem.at[block])

    lax.fori_loop(0, blocks, lambda block, _: load(block).start(), None)
    o_ref[...] = near_ref[...] * scale

    def add(block, _):
        load(block).wait()
        start = pl.multiple_of(block * FAR_BLOCK, FAR_BLOCK)
        far = held[pl.ds(start, FAR_BLOCK), :] * scale
        high = far.astype(BF16)
        low = (far - high.astype(F32)).astype(BF16)
        spread = spread_ref[:, pl.ds(start, FAR_BLOCK)]
        o_ref[...] += dot(spread, high) + dot(spread, low)

    lax.fori_loop(0, blocks, add, None)


def merge_kernel(scale, mine_ref, *refs):
    total = mine_ref[...]
    for spread_ref, back_ref in zip(refs[0:-1:2], refs[1:-1:2]):
        total = total + dot(spread_ref[...], back_ref[...]) * scale
    refs[-1][...] = total


def params():
    return dict(
        compiler_params=pltpu.CompilerParams(vmem_limit_bytes=VMEM_BYTES),
        cost_estimate=pl.CostEstimate(flops=1000, bytes_accessed=1000, transcendentals=0),
    )


def whole(shape):
    return pl.BlockSpec(shape, lambda *_: (0,) * len(shape))


def prepare(spectra, info, width, counts, pairs, live):
    rows, windows, two, bins = spectra.shape
    parts = windows * two
    lanes = [parts * bins] + [parts * pieces * width for pieces in counts]
    blocks = [pl.BlockSpec((ROW_BLOCK, n), lambda i, s: (i, 0)) for n in lanes]
    shapes = [jax.ShapeDtypeStruct((rows, n), BF16) for n in lanes]
    return pl.pallas_call(
        functools.partial(prepare_kernel, width, counts),
        grid_spec=pltpu.PrefetchScalarGridSpec(
            num_scalar_prefetch=1,
            grid=(rows // ROW_BLOCK,),
            in_specs=[
                pl.BlockSpec((ROW_BLOCK, windows, two, bins), lambda i, s: (i, 0, 0, 0)),
                whole(pairs.shape),
                whole(live.shape),
            ],
            out_specs=blocks[:1] + [whole((windows, two, bins + live.shape[1]))] + blocks[1:],
        ),
        out_shape=shapes[:1] + [jax.ShapeDtypeStruct((windows, two, bins + live.shape[1]), F32)]
        + shapes[1:],
        name="prepare",
        **params(),
    )(info, spectra, pairs, live)


def behind(array, *after):
    anywhere = pl.BlockSpec(memory_space=pl.ANY)
    return pl.pallas_call(
        lambda *refs: None,
        in_specs=[anywhere] * (1 + len(after)),
        out_specs=anywhere,
        out_shape=jax.ShapeDtypeStruct(array.shape, array.dtype),
        input_output_aliases={0: 0},
        name="behind",
        **params(),
    )(array, *after)


def body(spectra, pair_channels, pair_live):
    rows, windows, _, bins = spectra.shape
    parts = 2 * windows
    count = lax.axis_size("row")
    me = lax.axis_index("row")
    odd = me % 2
    first_row = me * rows
    half = bins // 2
    fast = [(i, i ^ 1) for i in range(count)]
    slow = [(i, i + 1) for i in range(1, count - 1, 2)]
    slow = slow + [(b, a) for a, b in slow]
    piece = half // 4
    send_start = (1 - odd) * half

    tiles, tile = pair_live.shape
    slots = tiles * tile
    first_rows = pair_channels[:, :, 0] - first_row
    offsets = pair_channels[:, :, 1] - first_row
    code = jnp.concatenate([first_rows, offsets - first_rows, pair_live], axis=0).astype(BF16)
    code_rows = -(-3 * tiles // 16) * 16
    code = jnp.pad(code, ((0, code_rows - 3 * tiles), (0, 0)))
    far_code = lax.ppermute(code, "row", slow)

    counts = (1, 1, 1, 1)
    far_low = first_row + jnp.where(odd == 1, rows, -rows)
    flat, total, *chunks = prepare(
        spectra,
        jnp.stack([send_start, far_low, jnp.int32(rows)]),
        piece,
        counts,
        jnp.swapaxes(pair_channels, 1, 2),
        pair_live,
    )
    if count & (count - 1):
        reach = lax.psum(total, "row")
        partner_rows = lax.ppermute(flat, "row", fast)
        far_rows = [lax.ppermute(behind(chunks[0], reach, far_code), "row", slow)]
    else:
        reach = total
        jump = 1
        while jump < count:
            others = [
                lax.ppermute(reach, "row", [(i, i ^ k) for i in range(count)])
                for k in (jump, 2 * jump, 3 * jump)
                if 2 * jump < count or k == jump
            ]
            reach = functools.reduce(jnp.add, others, reach)
            if jump == 1:
                flat = behind(flat, reach)
                partner_rows = lax.ppermute(flat, "row", fast)
                far_rows = [lax.ppermute(behind(chunks[0], reach, far_code), "row", slow)]
            jump *= 4
    common = reach / (rows * count)
    far_rows.append(lax.ppermute(behind(chunks[1], reach), "row", slow))
    far_rows.append(lax.ppermute(behind(chunks[2], partner_rows), "row", slow))

    wide = NEAR_GROUPS * GROUP
    near_shift = jnp.where(odd == 1, -rows, rows)
    order = jnp.arange(slots, dtype=jnp.int32).reshape(tiles, tile)
    live_end = jnp.max(jnp.where(pair_live != 0, order + 1, 0))
    near_info = jnp.stack(
        [near_shift, live_end, odd * (half // wide), (1 - odd) * (half // wide)]
    )
    lists = (first_rows, offsets, pair_live)
    list_specs = [whole((tiles, tile))] * 3
    table = jnp.asarray(lag_table(bins, LAGS))
    mean = jnp.asarray(band_mean())

    steps = bins // wide
    share = half // wide

    def near_call(first, before):
        offset = 2 if first else 3

        def bin_block(j, s):
            return s[offset] + j

        return pl.pallas_call(
            functools.partial(near_kernel, parts, first),
            grid_spec=pltpu.PrefetchScalarGridSpec(
                num_scalar_prefetch=1,
                grid=(share,),
                in_specs=[
                    pl.BlockSpec(
                        (rows, wide),
                        functools.partial(lambda p, j, s: (0, p * steps + bin_block(j, s)), p),
                    )
                    for _ in range(2)
                    for p in range(parts)
                ]
                + [
                    pl.BlockSpec((windows, 2, wide), lambda j, s: (0, 0, bin_block(j, s))),
                    pl.BlockSpec((2, wide, LAGS), lambda j, s: (0, bin_block(j, s), 0)),
                    whole((GROUP, GROUP)),
                ]
                + list_specs
                + [pl.BlockSpec(memory_space=pl.ANY) if first else whole((slots, LAGS))],
                out_specs=[whole((slots, LAGS))]
                + [pl.BlockSpec((rows, wide), lambda j, s: (0, j))] * (parts * first),
                scratch_shapes=[pltpu.VMEM((slots, 2 * rows), BF16)] * 2
                + [pltpu.VMEM((2 * rows, parts * GROUP), BF16)] * NEAR_GROUPS,
            ),
            out_shape=[jax.ShapeDtypeStruct((slots, LAGS), F32)]
            + [jax.ShapeDtypeStruct((rows, half), BF16)] * (parts * first),
            name="near_pairs",
            **params(),
        )(
            near_info,
            *[flat] * parts,
            *[partner_rows] * parts,
            common,
            table,
            mean,
            *lists,
            before,
        )

    near_acc, *white = near_call(True, far_code)
    far_rows.append(lax.ppermute(behind(chunks[3], near_acc), "row", slow))
    (near_acc,) = near_call(False, near_acc)

    hot_a, hot_b, spread, back_spread, rest_spread, cross_count = pl.pallas_call(
        plan_kernel,
        grid_spec=pltpu.PrefetchScalarGridSpec(
            num_scalar_prefetch=1,
            grid=(1,),
            in_specs=list_specs
            + [whole((code_rows, tile))]
            + [pl.BlockSpec(memory_space=pl.ANY)],
            out_specs=[
                whole((2 * slots, 2 * rows)),
                whole((2 * slots, 2 * rows)),
                whole((slots, 2 * slots)),
                whole((slots, BACK_ROWS)),
                whole((slots, slots - BACK_ROWS)),
                pl.BlockSpec(memory_space=pltpu.SMEM),
            ],
        ),
        out_shape=[
            jax.ShapeDtypeStruct((2 * slots, 2 * rows), BF16),
            jax.ShapeDtypeStruct((2 * slots, 2 * rows), BF16),
            jax.ShapeDtypeStruct((slots, 2 * slots), BF16),
            jax.ShapeDtypeStruct((slots, BACK_ROWS), BF16),
            jax.ShapeDtypeStruct((slots, slots - BACK_ROWS), BF16),
            jax.ShapeDtypeStruct((1,), jnp.int32),
        ],
        name="plan",
        **params(),
    )(-near_shift[None], *lists, far_code, near_acc)

    info = (odd * (half // piece))[None]

    owned = [(k, n, i) for k, n in enumerate(counts) for i in range(n)]

    def far_call(at, first, before):
        pieces = len(at)
        own_at = [functools.partial(lambda c, j, s, n: s[0] + c, c) for c in at]
        specs = (
            [
                pl.BlockSpec((rows, piece), functools.partial(lambda n, *i: (0, n), c))
                for c in at
                for _ in range(parts)
            ]
            + [
                pl.BlockSpec((rows, piece), functools.partial(lambda n, *i: (0, n), p * owned[c][1] + owned[c][2]))
                for c in at
                for p in range(parts)
            ]
            + [
                pl.BlockSpec((windows, 2, piece), functools.partial(lambda f, *i: (0, 0, f(*i)), f))
                for f in own_at
            ]
            + [
                pl.BlockSpec((2, piece, LAGS), functools.partial(lambda f, *i: (0, f(*i), 0), f))
                for f in own_at
            ]
            + [whole((GROUP, GROUP))]
            + [whole((2 * slots, 2 * rows))] * 2
        )
        operands = (
            list(white) * pieces
            + [far_rows[owned[c][0]] for c in at for _ in range(parts)]
            + [common] * pieces
            + [table] * pieces
            + [mean, hot_a, hot_b]
        )
        out_specs = [pl.BlockSpec(memory_space=pl.ANY)]
        out_shape = [jax.ShapeDtypeStruct((2 * slots, LAGS), F32)]
        specs.append(pl.BlockSpec(memory_space=pl.ANY))
        operands.append(before)
        if not first:
            for back_rows in (BACK_ROWS, slots - BACK_ROWS):
                out_specs.append(whole((back_rows, LAGS)))
                out_shape.append(jax.ShapeDtypeStruct((back_rows, LAGS), BF16))
        most = 2 * slots // FAR_BLOCK
        return pl.pallas_call(
            functools.partial(far_kernel, parts, pieces, first),
            grid_spec=pltpu.PrefetchScalarGridSpec(
                num_scalar_prefetch=2,
                grid=(1,),
                in_specs=specs,
                out_specs=out_specs,
                scratch_shapes=[
                    pltpu.VMEM((2 * slots, LAGS), F32),
                    pltpu.SemaphoreType.DMA((most,)),
                    pltpu.SemaphoreType.DMA((most,)),
                ]
                + [pltpu.VMEM((2 * rows, parts * GROUP), BF16)] * (pieces * piece // GROUP),
            ),
            out_shape=out_shape,
            name="far_pairs",
            **params(),
        )(info, cross_count, *operands)

    (before,) = far_call((0, 1, 2), True, near_acc)
    far_acc, theirs, their_rest = far_call((3,), False, before)

    scale = 1.0 / math.sqrt(bins * windows)
    back = lax.ppermute(theirs, "row", slow)
    gathered = pl.pallas_call(
        functools.partial(gather_kernel, scale),
        grid_spec=pltpu.PrefetchScalarGridSpec(
            num_scalar_prefetch=1,
            grid=(1,),
            in_specs=[
                whole((slots, LAGS)),
                whole((slots, 2 * slots)),
                pl.BlockSpec(memory_space=pl.ANY),
            ],
            out_specs=whole((slots, LAGS)),
            scratch_shapes=[
                pltpu.VMEM((2 * slots, LAGS), F32),
                pltpu.SemaphoreType.DMA((2 * slots // FAR_BLOCK,)),
            ],
        ),
        out_shape=jax.ShapeDtypeStruct((slots, LAGS), F32),
        name="gather",
        **params(),
    )(cross_count, near_acc, spread, far_acc)

    def merge(*spread_back):
        return pl.pallas_call(
            functools.partial(merge_kernel, scale),
            grid=(tiles,),
            in_specs=[pl.BlockSpec((tile, LAGS), lambda i: (i, 0))]
            + [
                spec
                for k in range(0, len(spread_back), 2)
                for spec in (
                    pl.BlockSpec((tile, spread_back[k].shape[1]), lambda i: (i, 0)),
                    whole(spread_back[k + 1].shape),
                )
            ],
            out_specs=pl.BlockSpec((tile, LAGS), lambda i: (i, 0)),
            out_shape=jax.ShapeDtypeStruct((slots, LAGS), F32),
            name="merge",
            **params(),
        )(gathered, *spread_back)

    result = lax.cond(
        common[0, 0, bins] > 0,
        lambda: merge(back_spread, back, rest_spread, lax.ppermute(their_rest, "row", slow)),
        lambda: merge(back_spread, back),
    )
    return result.reshape(pair_live.shape + (LAGS,))


def solution(mesh):
    placed = (P(("day", "row"), None, None, None), P("row", None, None), P("row", None))
    return jax.shard_map(
        body, mesh=mesh, in_specs=placed, out_specs=P(("day", "row"), None, None), check_vma=False
    )
```

```python
import functools
import math

import jax
import jax.numpy as jnp
import numpy as np
from jax import lax
from jax.experimental import pallas as pl
from jax.experimental.pallas import tpu as pltpu
from jax.sharding import PartitionSpec as P

BAND = 64
LAGS = 512
GROUP = 256
NEAR_GROUPS = 4
FAR_BLOCK = 256
BACK_ROWS = 160
ROW_BLOCK = 16
TINY = 1e-37
VMEM_BYTES = 56 * 1024 * 1024
F32 = jnp.float32
BF16 = jnp.bfloat16


def lag_table(bins, lags):
    shifts = np.arange(lags, dtype=np.int64)[None, :] - lags // 2
    phase = np.mod(np.arange(bins, dtype=np.int64)[:, None] * shifts, 2 * bins)
    angle = (phase.astype(np.float32) * np.float32(math.pi / bins)).astype(np.float64)
    both = np.stack([np.cos(angle), -np.sin(angle)]).astype(np.float32)
    return both.astype(jnp.bfloat16)


def band_mean():
    rows = np.arange(GROUP)[:, None] // BAND
    cols = np.arange(GROUP)[None, :] // BAND
    return np.where(rows == cols, 1.0 / BAND, 0.0).astype(jnp.bfloat16)


def dot(a, b):
    return jnp.dot(a, b, preferred_element_type=F32)


def whiten_into(w_ref, row0, raws, common_ref, mean_ref, start):
    rows = raws[0].shape[0]
    target = pl.ds(row0, rows)
    cols = pl.ds(start, GROUP)
    for w in range(len(raws) // 2):
        re = raws[2 * w][:, cols].astype(F32) - common_ref[w, 0:1, cols]
        im = raws[2 * w + 1][:, cols].astype(F32) - common_ref[w, 1:2, cols]
        power = re * re + im * im
        magnitude = (power * lax.rsqrt(jnp.maximum(power, TINY))).astype(BF16)
        scale = 1.0 / (dot(magnitude, mean_ref[...]) + 1e-06)
        w_ref[target, pl.ds(2 * w * GROUP, GROUP)] = (re * scale).astype(BF16)
        w_ref[target, pl.ds((2 * w + 1) * GROUP, GROUP)] = (im * scale).astype(BF16)


def columns_of(rows_of_tiles):
    lanes = rows_of_tiles.shape[1]
    padded = rows_of_tiles.astype(F32)
    if missing := -padded.shape[0] % 8:
        padded = jnp.concatenate([padded, jnp.zeros((missing, lanes), F32)], axis=0)
    square = (lanes, lanes)
    same = lax.broadcasted_iota(jnp.int32, square, 0) == lax.broadcasted_iota(jnp.int32, square, 1)
    unit = jnp.where(same, 1.0, 0.0).astype(BF16)
    return lax.dot_general(
        unit, padded.astype(BF16), (((1,), (1,)), ((), ())), preferred_element_type=F32
    )


def hot_rows(column, width):
    lane = lax.broadcasted_iota(jnp.int32, (column.shape[0], width), 1).astype(F32)
    return jnp.where(column == lane, 1.0, 0.0).astype(BF16)


def fill_hot(values, hot_ref):
    tiles, lanes = values.shape
    columns = columns_of(values)
    for tile in range(tiles):
        hot_ref[pl.ds(tile * lanes, lanes), :] = hot_rows(
            columns[:, tile : tile + 1], hot_ref.shape[1]
        )


def correlate_rows(hot_a, hot_b, w_ref, table_ref, start):
    both = dot(jnp.concatenate([hot_a, hot_b], axis=0), w_ref[...])
    a, b = both[: hot_a.shape[0]], both[hot_a.shape[0] :]
    real = imag = None
    for w in range(w_ref.shape[1] // (2 * GROUP)):
        ar, ai, br, bi = (
            x[:, (2 * w + r) * GROUP : (2 * w + r + 1) * GROUP] for x in (a, b) for r in range(2)
        )
        re = ar * br + ai * bi
        im = ai * br - ar * bi
        real = re if real is None else real + re
        imag = im if imag is None else imag + im
    rows = pl.ds(start, GROUP)
    return dot(real.astype(BF16), table_ref[0, rows, :]) + dot(
        imag.astype(BF16), table_ref[1, rows, :]
    )


def near_kernel(parts, info_ref, *refs):
    refs = list(refs)

    def take(number):
        taken = refs[:number]
        del refs[:number]
        return taken

    own, other = take(parts), take(parts)
    common_ref, table_ref, mean_ref, first_ref, offset_ref, live_ref = take(6)
    (acc_ref,) = take(1)
    white = take(parts)
    hot_a, hot_b, *held = refs
    rows = own[0].shape[0]

    @pl.when(pl.program_id(0) == 0)
    def _():
        acc_ref[...] = jnp.zeros_like(acc_ref)
        shift = info_ref[0]
        offset = offset_ref[...]
        live = live_ref[...] != 0
        inside = (offset >= 0) & (offset < rows)
        beside = (offset >= shift) & (offset < shift + rows)
        place = jnp.where(inside, offset, jnp.where(beside, offset - shift + rows, -1))
        fill_hot(jnp.where(live, first_ref[...], -1), hot_a)
        fill_hot(jnp.where(live, place, -1), hot_b)

    def prepare(group):
        start = group * GROUP
        w_ref = held[group]
        whiten_into(w_ref, 0, own, common_ref, mean_ref, start)
        whiten_into(w_ref, rows, other, common_ref, mean_ref, start)
        for part in range(len(white)):
            white[part][:, pl.ds(start, GROUP)] = w_ref[
                pl.ds(0, rows), pl.ds(part * GROUP, GROUP)
            ]

    def run(block):
        slots = pl.ds(0, block)
        prepare(0)
        for group in range(len(held)):
            if group + 1 < len(held):
                prepare(group + 1)
            acc_ref[slots, :] += correlate_rows(
                hot_a[slots, :], hot_b[slots, :], held[group], table_ref, group * GROUP
            )

    total = hot_a.shape[0]
    pl.when(info_ref[1] <= total // 2)(lambda: run(total // 2))
    pl.when(info_ref[1] > total // 2)(lambda: run(total))


def plan_kernel(info_ref, first_ref, offset_ref, live_ref, code_ref, flag_ref, _, hot_a, hot_b, spread, back, rest, count_ref):
    tiles, lanes = first_ref.shape
    rows = hot_a.shape[1] // 2
    shift = info_ref[0]
    code = code_ref[...].astype(F32).astype(jnp.int32)
    far_a = code[0:tiles]
    far_b = far_a + code[tiles : 2 * tiles] + shift
    theirs = (far_b >= 0) & (far_b < rows) & (code[2 * tiles : 3 * tiles] != 0)
    offset = offset_ref[...]
    owns = (offset >= shift) & (offset < shift + rows) & (live_ref[...] != 0)
    cross = jnp.concatenate([theirs.astype(F32), owns.astype(F32)], axis=0)
    values_a = jnp.concatenate([far_a + rows, first_ref[...]], axis=0)
    values_b = jnp.concatenate([far_b, offset - shift + rows], axis=0)
    square = (lanes, lanes)
    row = lax.broadcasted_iota(jnp.int32, square, 0)
    col = lax.broadcasted_iota(jnp.int32, square, 1)
    ahead = jnp.where(row < col, 1.0, 0.0).astype(BF16)
    within = dot(cross.astype(BF16), ahead)
    sums = jnp.sum(cross, axis=1, keepdims=True)
    slots = hot_a.shape[0]
    packed = lax.broadcasted_iota(jnp.int32, (slots, lanes), 0).astype(F32)
    lane_rows = lax.broadcasted_iota(jnp.int32, (2 * rows, lanes), 0)
    base = jnp.zeros((1, 1), F32)
    total_a = jnp.zeros(hot_a.shape, F32)
    total_b = jnp.zeros(hot_b.shape, F32)
    bases = []
    for tile in range(2 * tiles):
        bases.append(base)
        place = jnp.where(cross[tile : tile + 1] > 0, within[tile : tile + 1] + base, -1.0)
        select = jnp.where(packed == place, 1.0, 0.0).astype(BF16)
        for values, which in ((values_a, 0), (values_b, 1)):
            ones = jnp.where(lane_rows == values[tile : tile + 1], 1.0, 0.0).astype(BF16)
            part = lax.dot_general(
                select, ones, (((1,), (1,)), ((), ())), preferred_element_type=F32
            )
            if which:
                total_b = total_b + part
            else:
                total_a = total_a + part
        base = base + sums[tile : tile + 1]
    hot_a[...] = total_a.astype(BF16)
    hot_b[...] = total_b.astype(BF16)
    within_columns = columns_of(within)
    cross_columns = columns_of(cross)
    for tile in range(tiles):
        mine = tiles + tile
        live_column = cross_columns[:, mine : mine + 1] > 0
        column = within_columns[:, mine : mine + 1] + bases[mine]
        target = pl.ds(tile * lanes, lanes)
        spread[target, :] = hot_rows(jnp.where(live_column, column, -1.0), spread.shape[1])
        column = jnp.where(live_column, column - bases[tiles], -1.0)
        back[target, :] = hot_rows(column, back.shape[1])
        rest[target, :] = hot_rows(column - back.shape[1], rest.shape[1])
    count_ref[0] = jnp.sum(cross).astype(jnp.int32)
    count_ref[1] = (jnp.max(flag_ref[...]) > 0).astype(jnp.int32)


def far_kernel(parts, first, info_ref, count_ref, *refs):
    refs = list(refs)

    def take(number):
        taken = refs[:number]
        del refs[:number]
        return taken

    white = take(parts)
    direct = take(parts)
    across = take(parts) if first else direct
    common_ref, table_ref, mean_ref, hot_a, hot_b, before_ref, acc_ref = take(7)
    sent_ref, rest_ref = (None, None) if first else take(2)
    held = refs
    rows = direct[0].shape[0]
    step = pl.program_id(0)
    blocks = (count_ref[0] + FAR_BLOCK - 1) // FAR_BLOCK

    for group, w_ref in enumerate(held):
        start = group * GROUP
        for part in range(parts):
            w_ref[pl.ds(0, rows), pl.ds(part * GROUP, GROUP)] = white[part][
                :, pl.ds(start, GROUP)
            ]
        if first:
            pl.when(info_ref[1] == 0)(
                lambda: whiten_into(w_ref, rows, direct, common_ref, mean_ref, start)
            )
            pl.when(info_ref[1] != 0)(
                lambda: whiten_into(w_ref, rows, across, common_ref, mean_ref, start)
            )
        else:
            whiten_into(w_ref, rows, direct, common_ref, mean_ref, start)

    def one_block(block, _):
        target = pl.ds(pl.multiple_of(block * FAR_BLOCK, FAR_BLOCK), FAR_BLOCK)
        gained = None
        for group, w_ref in enumerate(held):
            part = correlate_rows(
                hot_a[target, :], hot_b[target, :], w_ref, table_ref, group * GROUP
            )
            gained = part if gained is None else gained + part

        @pl.when(step == 0)
        def _():
            acc_ref[target, :] = gained if first else before_ref[target, :] + gained

        @pl.when(step > 0)
        def _():
            acc_ref[target, :] += gained

    lax.fori_loop(0, blocks, one_block, None)

    @pl.when((step == pl.num_programs(0) - 1) & (not first))
    def _():
        if first:
            return
        sent = sent_ref.shape[0]
        used = lax.broadcasted_iota(jnp.int32, (sent + rest_ref.shape[0], 1), 0)
        used = used < blocks * FAR_BLOCK
        for ref, at in ((sent_ref, 0), (rest_ref, sent)):
            ours = slice(at, at + ref.shape[0])
            ref[...] = jnp.where(used[ours], acc_ref[ours, :], 0.0).astype(BF16)


def prepare_kernel(width, counts, info_ref, x_ref, pairs_ref, live_ref, flat_ref, total_ref, code_ref, *sent):
    bins = x_ref.shape[3]
    parts = flat_ref.shape[1] // bins
    flat_ref[...] = x_ref[...].reshape(flat_ref.shape)
    total = x_ref[0].astype(F32)
    for row in range(1, x_ref.shape[0]):
        total = total + x_ref[row].astype(F32)

    @pl.when(pl.program_id(0) == 0)
    def _():
        total_ref[:, :, pl.ds(0, bins)] = total
        pairs = pairs_ref[...]
        live = live_ref[...]
        listed = [pairs[:, 0, :] - info_ref[3], pairs[:, 1, :] - pairs[:, 0, :], live]
        spare = code_ref.shape[0] - 3 * live.shape[0]
        if spare:
            listed.append(jnp.zeros((spare, live.shape[1]), jnp.int32))
        code_ref[...] = jnp.concatenate(listed, axis=0).astype(F32).astype(BF16)
        second = pairs[:, 1, :] - info_ref[1]
        crossing = (second >= 0) & (second < info_ref[2]) & (live_ref[...] != 0)
        number = jnp.sum(jnp.where(crossing, 1.0, 0.0))
        flag = jnp.where(number > BACK_ROWS, 1.0, 0.0)
        lanes = total_ref.shape[2] - bins
        total_ref[:, :, pl.ds(bins, lanes)] = jnp.full(total_ref.shape[:2] + (lanes,), flag, F32)

    @pl.when(pl.program_id(0) > 0)
    def _():
        total_ref[:, :, pl.ds(0, bins)] += total

    done = 0
    for pieces, ref in zip(counts, sent):
        for part in range(parts):
            start = part * bins + done * width + info_ref[0]
            ref[:, pl.ds(part * pieces * width, pieces * width)] = flat_ref[
                :, pl.ds(pl.multiple_of(start, width), pieces * width)
            ]
        done += pieces


def gather_kernel(scale, count_ref, near_ref, spread_ref, far_ref, o_ref, held, sem):
    blocks = (count_ref[0] + FAR_BLOCK - 1) // FAR_BLOCK

    def load(block):
        rows = pl.ds(pl.multiple_of(block * FAR_BLOCK, FAR_BLOCK), FAR_BLOCK)
        return pltpu.make_async_copy(far_ref.at[rows, :], held.at[rows, :], sem.at[block])

    lax.fori_loop(0, blocks, lambda block, _: load(block).start(), None)
    o_ref[...] = near_ref[...] * scale

    def add(block, _):
        load(block).wait()
        start = pl.multiple_of(block * FAR_BLOCK, FAR_BLOCK)
        far = held[pl.ds(start, FAR_BLOCK), :] * scale
        high = far.astype(BF16)
        low = (far - high.astype(F32)).astype(BF16)
        spread = spread_ref[:, pl.ds(start, FAR_BLOCK)]
        o_ref[...] += dot(spread, high) + dot(spread, low)

    lax.fori_loop(0, blocks, add, None)


def merge_kernel(scale, mine_ref, *refs):
    total = mine_ref[...]
    for spread_ref, back_ref in zip(refs[0:-1:2], refs[1:-1:2]):
        total = total + dot(spread_ref[...], back_ref[...]) * scale
    refs[-1][...] = total


def params():
    return dict(
        compiler_params=pltpu.CompilerParams(vmem_limit_bytes=VMEM_BYTES),
        cost_estimate=pl.CostEstimate(flops=1000, bytes_accessed=1000, transcendentals=0),
    )


def whole(shape):
    return pl.BlockSpec(shape, lambda *_: (0,) * len(shape))


def prepare(spectra, info, width, counts, pairs, live):
    rows, windows, two, bins = spectra.shape
    parts = windows * two
    code_rows = -(-3 * live.shape[0] // 16) * 16
    lanes = [parts * bins] + [parts * pieces * width for pieces in counts]
    blocks = [pl.BlockSpec((ROW_BLOCK, n), lambda i, s: (i, 0)) for n in lanes]
    shapes = [jax.ShapeDtypeStruct((rows, n), BF16) for n in lanes]
    return pl.pallas_call(
        functools.partial(prepare_kernel, width, counts),
        grid_spec=pltpu.PrefetchScalarGridSpec(
            num_scalar_prefetch=1,
            grid=(rows // ROW_BLOCK,),
            in_specs=[
                pl.BlockSpec((ROW_BLOCK, windows, two, bins), lambda i, s: (i, 0, 0, 0)),
                whole(pairs.shape),
                whole(live.shape),
            ],
            out_specs=blocks[:1]
            + [whole((windows, two, bins + live.shape[1])), whole((code_rows, live.shape[1]))]
            + blocks[1:],
        ),
        out_shape=shapes[:1] + [jax.ShapeDtypeStruct((windows, two, bins + live.shape[1]), F32)]
        + [jax.ShapeDtypeStruct((code_rows, live.shape[1]), BF16)]
        + shapes[1:],
        name="prepare",
        **params(),
    )(info, spectra, pairs, live)


def behind(array, *after):
    anywhere = pl.BlockSpec(memory_space=pl.ANY)
    return pl.pallas_call(
        lambda *refs: None,
        in_specs=[anywhere] * (1 + len(after)),
        out_specs=anywhere,
        out_shape=jax.ShapeDtypeStruct(array.shape, array.dtype),
        input_output_aliases={0: 0},
        name="behind",
        **params(),
    )(array, *after)


def body(spectra, pair_channels, pair_live):
    rows, windows, _, bins = spectra.shape
    parts = 2 * windows
    count = lax.axis_size("row")
    me = lax.axis_index("row")
    odd = me % 2
    first_row = me * rows
    half = bins // 2
    fast = [(i, i ^ 1) for i in range(count)]

    def slow_of(*places):
        up = [(i, i + 1) for i in range(1, count - 1, 2) if i % 4 in places]
        return up + [(b, a) for a, b in up]

    slow = slow_of(1, 3)
    piece = half // 4
    send_start = (1 - odd) * half

    tiles, tile = pair_live.shape
    slots = tiles * tile
    first_rows = pair_channels[:, :, 0] - first_row
    offsets = pair_channels[:, :, 1] - first_row
    counts = (2, 2)
    far_low = first_row + jnp.where(odd == 1, rows, -rows)
    flat, total, code, *chunks = prepare(
        spectra,
        jnp.stack([send_start, far_low, jnp.int32(rows), first_row]),
        piece,
        counts,
        jnp.swapaxes(pair_channels, 1, 2),
        pair_live,
    )
    far_code = lax.ppermute(code, "row", slow)
    if count & (count - 1):
        far_direct = lax.ppermute(chunks[0], "row", slow_of(1))
        reach = lax.psum(total, "row")
        partner_rows = lax.ppermute(flat, "row", fast)
    else:
        reach = total
        jump = 1
        while jump < count:
            others = [
                lax.ppermute(reach, "row", [(i, i ^ k) for i in range(count)])
                for k in (jump, 2 * jump, 3 * jump)
                if 2 * jump < count or k == jump
            ]
            reach = functools.reduce(jnp.add, others, reach)
            if jump == 1:
                reach = behind(reach, far_code)
                far_direct = lax.ppermute(behind(chunks[0], reach), "row", slow_of(1))
                flat = behind(flat, reach)
                partner_rows = lax.ppermute(flat, "row", fast)
            jump *= 4
    common = reach / (rows * count)
    far_across = lax.ppermute(behind(chunks[0], reach), "row", slow_of(3))
    far_second = lax.ppermute(behind(chunks[1], reach), "row", slow)

    wide = NEAR_GROUPS * GROUP
    near_shift = jnp.where(odd == 1, -rows, rows)
    order = jnp.arange(slots, dtype=jnp.int32).reshape(tiles, tile)
    live_end = jnp.max(jnp.where(pair_live != 0, order + 1, 0))
    near_info = jnp.stack(
        [near_shift, live_end, odd * (half // wide)]
    )
    lists = (first_rows, offsets, pair_live)
    list_specs = [whole((tiles, tile))] * 3
    table = jnp.asarray(lag_table(bins, LAGS))
    mean = jnp.asarray(band_mean())

    steps = bins // wide

    def near_call():
        def bin_block(j, s):
            return lax.rem(s[2] + j, steps)

        return pl.pallas_call(
            functools.partial(near_kernel, parts),
            grid_spec=pltpu.PrefetchScalarGridSpec(
                num_scalar_prefetch=1,
                grid=(steps,),
                in_specs=[
                    pl.BlockSpec(
                        (rows, wide),
                        functools.partial(lambda p, j, s: (0, p * steps + bin_block(j, s)), p),
                    )
                    for _ in range(2)
                    for p in range(parts)
                ]
                + [
                    pl.BlockSpec((windows, 2, wide), lambda j, s: (0, 0, bin_block(j, s))),
                    pl.BlockSpec((2, wide, LAGS), lambda j, s: (0, bin_block(j, s), 0)),
                    whole((GROUP, GROUP)),
                ]
                + list_specs,
                out_specs=[whole((slots, LAGS))]
                + [pl.BlockSpec((rows, wide), lambda j, s: (0, j))] * parts,
                scratch_shapes=[pltpu.VMEM((slots, 2 * rows), BF16)] * 2
                + [pltpu.VMEM((2 * rows, parts * GROUP), BF16)] * NEAR_GROUPS,
            ),
            out_shape=[jax.ShapeDtypeStruct((slots, LAGS), F32)]
            + [jax.ShapeDtypeStruct((rows, bins), BF16)] * parts,
            name="near_pairs",
            **params(),
        )(
            near_info,
            *[flat] * parts,
            *[partner_rows] * parts,
            common,
            table,
            mean,
            *lists,
        )

    near_acc, *white = near_call()

    hot_a, hot_b, spread, back_spread, rest_spread, cross_count = pl.pallas_call(
        plan_kernel,
        grid_spec=pltpu.PrefetchScalarGridSpec(
            num_scalar_prefetch=1,
            grid=(1,),
            in_specs=list_specs
            + [whole(code.shape)]
            + [pl.BlockSpec((windows, 2, tile), lambda j, s: (0, 0, bins // tile))]
            + [pl.BlockSpec(memory_space=pl.ANY)],
            out_specs=[
                whole((2 * slots, 2 * rows)),
                whole((2 * slots, 2 * rows)),
                whole((slots, 2 * slots)),
                whole((slots, BACK_ROWS)),
                whole((slots, slots - BACK_ROWS)),
                pl.BlockSpec(memory_space=pltpu.SMEM),
            ],
        ),
        out_shape=[
            jax.ShapeDtypeStruct((2 * slots, 2 * rows), BF16),
            jax.ShapeDtypeStruct((2 * slots, 2 * rows), BF16),
            jax.ShapeDtypeStruct((slots, 2 * slots), BF16),
            jax.ShapeDtypeStruct((slots, BACK_ROWS), BF16),
            jax.ShapeDtypeStruct((slots, slots - BACK_ROWS), BF16),
            jax.ShapeDtypeStruct((2,), jnp.int32),
        ],
        name="plan",
        **params(),
    )(-near_shift[None], *lists, far_code, common, near_acc)

    across = (((me + 1) // 2) % 2 == 0).astype(jnp.int32)
    info = jnp.stack([odd * (half // piece), across])

    def far_call(first, arrays, before):
        pieces = half // piece // 2
        base = 0 if first else pieces
        choose = (lambda s, k: s[1] == k) if first else (lambda s, k: True)
        back_rows = () if first else (BACK_ROWS, slots - BACK_ROWS)
        return pl.pallas_call(
            functools.partial(far_kernel, parts, first),
            grid_spec=pltpu.PrefetchScalarGridSpec(
                num_scalar_prefetch=2,
                grid=(pieces,),
                in_specs=[
                    pl.BlockSpec((rows, piece), lambda j, s, n: (0, base + j)) for _ in range(parts)
                ]
                + [
                    pl.BlockSpec(
                        (rows, piece),
                        functools.partial(
                            lambda k, p, j, s, n: (0, jnp.where(choose(s, k), p * pieces + j, 0)),
                            k,
                            p,
                        ),
                    )
                    for k in range(len(arrays))
                    for p in range(parts)
                ]
                + [
                    pl.BlockSpec((windows, 2, piece), lambda j, s, n: (0, 0, s[0] + base + j)),
                    pl.BlockSpec((2, piece, LAGS), lambda j, s, n: (0, s[0] + base + j, 0)),
                    whole((GROUP, GROUP)),
                    whole((2 * slots, 2 * rows)),
                    whole((2 * slots, 2 * rows)),
                    pl.BlockSpec(memory_space=pl.ANY) if first else whole((2 * slots, LAGS)),
                ],
                out_specs=[whole((2 * slots, LAGS))] + [whole((n, LAGS)) for n in back_rows],
                scratch_shapes=[pltpu.VMEM((2 * rows, parts * GROUP), BF16)] * (piece // GROUP),
            ),
            out_shape=[jax.ShapeDtypeStruct((2 * slots, LAGS), F32)]
            + [jax.ShapeDtypeStruct((n, LAGS), BF16) for n in back_rows],
            name="far_pairs",
            **params(),
        )(
            info,
            cross_count,
            *white,
            *[a for a in arrays for _ in range(parts)],
            common,
            table,
            mean,
            hot_a,
            hot_b,
            before,
        )

    (before,) = far_call(True, (far_direct, far_across), near_acc)
    far_acc, theirs, their_rest = far_call(False, (far_second,), before)

    scale = 1.0 / math.sqrt(bins * windows)
    back = lax.ppermute(theirs, "row", slow)
    gathered = pl.pallas_call(
        functools.partial(gather_kernel, scale),
        grid_spec=pltpu.PrefetchScalarGridSpec(
            num_scalar_prefetch=1,
            grid=(1,),
            in_specs=[
                whole((slots, LAGS)),
                whole((slots, 2 * slots)),
                pl.BlockSpec(memory_space=pl.ANY),
            ],
            out_specs=whole((slots, LAGS)),
            scratch_shapes=[
                pltpu.VMEM((2 * slots, LAGS), F32),
                pltpu.SemaphoreType.DMA((2 * slots // FAR_BLOCK,)),
            ],
        ),
        out_shape=jax.ShapeDtypeStruct((slots, LAGS), F32),
        name="gather",
        **params(),
    )(cross_count, near_acc, spread, far_acc)

    def merge(*spread_back):
        return pl.pallas_call(
            functools.partial(merge_kernel, scale),
            grid=(tiles,),
            in_specs=[pl.BlockSpec((tile, LAGS), lambda i: (i, 0))]
            + [
                spec
                for k in range(0, len(spread_back), 2)
                for spec in (
                    pl.BlockSpec((tile, spread_back[k].shape[1]), lambda i: (i, 0)),
                    whole(spread_back[k + 1].shape),
                )
            ],
            out_specs=pl.BlockSpec((tile, LAGS), lambda i: (i, 0)),
            out_shape=jax.ShapeDtypeStruct((slots, LAGS), F32),
            name="merge",
            **params(),
        )(gathered, *spread_back)

    result = lax.cond(
        cross_count[1] > 0,
        lambda: merge(back_spread, back, rest_spread, lax.ppermute(their_rest, "row", slow)),
        lambda: merge(back_spread, back),
    )
    return result.reshape(pair_live.shape + (LAGS,))


def solution(mesh):
    placed = (P(("day", "row"), None, None, None), P("row", None, None), P("row", None))
    return jax.shard_map(
        body, mesh=mesh, in_specs=placed, out_specs=P(("day", "row"), None, None), check_vma=False
    )
```

```python
import functools
import math

import jax
import jax.numpy as jnp
import numpy as np
from jax import lax
from jax.experimental import pallas as pl
from jax.experimental.pallas import tpu as pltpu
from jax.sharding import PartitionSpec as P

BAND = 64
LAGS = 512
GROUP = 256
NEAR_GROUPS = 4
FAR_BLOCK = 256
BACK_ROWS = 160
ROW_BLOCK = 16
TINY = 1e-37
F32 = jnp.float32
BF16 = jnp.bfloat16


def lag_table(bins, lags):
    shifts = np.arange(lags, dtype=np.int64)[None, :] - lags // 2
    phase = np.mod(np.arange(bins, dtype=np.int64)[:, None] * shifts, 2 * bins)
    angle = (phase.astype(np.float32) * np.float32(math.pi / bins)).astype(np.float64)
    both = np.stack([np.cos(angle), -np.sin(angle)]).astype(np.float32)
    return both.astype(jnp.bfloat16)


def band_mean():
    rows = np.arange(GROUP)[:, None] // BAND
    cols = np.arange(GROUP)[None, :] // BAND
    return np.where(rows == cols, 1.0 / BAND, 0.0).astype(jnp.bfloat16)


def dot(a, b):
    return jnp.dot(a, b, preferred_element_type=F32)


def whiten_into(w_ref, row0, raws, common_ref, mean_ref, start):
    rows = raws[0].shape[0]
    target = pl.ds(row0, rows)
    cols = pl.ds(start, GROUP)
    for w in range(len(raws) // 2):
        re = raws[2 * w][:, cols].astype(F32) - common_ref[w, 0:1, cols]
        im = raws[2 * w + 1][:, cols].astype(F32) - common_ref[w, 1:2, cols]
        power = re * re + im * im
        magnitude = (power * lax.rsqrt(jnp.maximum(power, TINY))).astype(BF16)
        scale = 1.0 / (dot(magnitude, mean_ref[...]) + 1e-06)
        w_ref[target, pl.ds(2 * w * GROUP, GROUP)] = (re * scale).astype(BF16)
        w_ref[target, pl.ds((2 * w + 1) * GROUP, GROUP)] = (im * scale).astype(BF16)


def columns_of(rows_of_tiles):
    lanes = rows_of_tiles.shape[1]
    padded = rows_of_tiles.astype(F32)
    if missing := -padded.shape[0] % 8:
        padded = jnp.concatenate([padded, jnp.zeros((missing, lanes), F32)], axis=0)
    square = (lanes, lanes)
    same = lax.broadcasted_iota(jnp.int32, square, 0) == lax.broadcasted_iota(jnp.int32, square, 1)
    unit = jnp.where(same, 1.0, 0.0).astype(BF16)
    return lax.dot_general(
        unit, padded.astype(BF16), (((1,), (1,)), ((), ())), preferred_element_type=F32
    )


def hot_rows(column, width):
    lane = lax.broadcasted_iota(jnp.int32, (column.shape[0], width), 1).astype(F32)
    return jnp.where(column == lane, 1.0, 0.0).astype(BF16)


def fill_hot(values, hot_ref):
    tiles, lanes = values.shape
    columns = columns_of(values)
    for tile in range(tiles):
        hot_ref[pl.ds(tile * lanes, lanes), :] = hot_rows(
            columns[:, tile : tile + 1], hot_ref.shape[1]
        )


def correlate_rows(hot_a, hot_b, w_ref, table_ref, start):
    both = dot(jnp.concatenate([hot_a, hot_b], axis=0), w_ref[...])
    a, b = both[: hot_a.shape[0]], both[hot_a.shape[0] :]
    real = imag = None
    for w in range(w_ref.shape[1] // (2 * GROUP)):
        ar, ai, br, bi = (
            x[:, (2 * w + r) * GROUP : (2 * w + r + 1) * GROUP] for x in (a, b) for r in range(2)
        )
        re = ar * br + ai * bi
        im = ai * br - ar * bi
        real = re if real is None else real + re
        imag = im if imag is None else imag + im
    rows = pl.ds(start, GROUP)
    return dot(real.astype(BF16), table_ref[0, rows, :]) + dot(
        imag.astype(BF16), table_ref[1, rows, :]
    )


def near_kernel(parts, info_ref, *refs):
    refs = list(refs)

    def take(number):
        taken = refs[:number]
        del refs[:number]
        return taken

    own, other = take(parts), take(parts)
    common_ref, table_ref, mean_ref, pairs_ref, live_ref, flag_ref, _ = take(7)
    (acc_ref,) = take(1)
    white = take(parts)
    (exceeds_ref,) = take(1)
    hot_a, hot_b, *held = refs
    rows = own[0].shape[0]

    @pl.when(pl.program_id(0) == 0)
    def _():
        acc_ref[...] = jnp.zeros_like(acc_ref)
        exceeds_ref[0] = (jnp.max(flag_ref[...]) > 0).astype(jnp.int32)
        lists = live_ref.shape
        order = lax.broadcasted_iota(jnp.int32, lists, 0) * lists[1]
        order = (order + lax.broadcasted_iota(jnp.int32, lists, 1) + 1).astype(F32)
        exceeds_ref[1] = jnp.max(jnp.where(live_ref[...] != 0, order, 0.0)).astype(jnp.int32)
        shift = info_ref[4]
        pairs = pairs_ref[...] - info_ref[3]
        offset = pairs[:, 1, :]
        live = live_ref[...] != 0
        inside = (offset >= 0) & (offset < rows)
        beside = (offset >= shift) & (offset < shift + rows)
        place = jnp.where(inside, offset, jnp.where(beside, offset - shift + rows, -1))
        fill_hot(jnp.where(live, pairs[:, 0, :], -1), hot_a)
        fill_hot(jnp.where(live, place, -1), hot_b)

    def prepare(group):
        start = group * GROUP
        w_ref = held[group]
        whiten_into(w_ref, 0, own, common_ref, mean_ref, start)
        whiten_into(w_ref, rows, other, common_ref, mean_ref, start)
        for part in range(len(white)):
            white[part][:, pl.ds(start, GROUP)] = w_ref[
                pl.ds(0, rows), pl.ds(part * GROUP, GROUP)
            ]

    def run(block):
        slots = pl.ds(0, block)
        prepare(0)
        for group in range(len(held)):
            if group + 1 < len(held):
                prepare(group + 1)
            acc_ref[slots, :] += correlate_rows(
                hot_a[slots, :], hot_b[slots, :], held[group], table_ref, group * GROUP
            )

    total = hot_a.shape[0]
    pl.when(exceeds_ref[1] <= total // 2)(lambda: run(total // 2))
    pl.when(exceeds_ref[1] > total // 2)(lambda: run(total))


def plan_kernel(info_ref, pairs_ref, live_ref, code_ref, _, hot_a, hot_b, spread, back, rest, count_ref):
    tiles, lanes = live_ref.shape
    rows = hot_a.shape[1] // 2
    shift = -info_ref[4]
    pairs = pairs_ref[...] - info_ref[3]
    code = code_ref[...].astype(F32).astype(jnp.int32)
    far_a = code[0:tiles]
    far_b = far_a + code[tiles : 2 * tiles] + shift
    theirs = (far_b >= 0) & (far_b < rows) & (code[2 * tiles : 3 * tiles] != 0)
    offset = pairs[:, 1, :]
    owns = (offset >= shift) & (offset < shift + rows) & (live_ref[...] != 0)
    cross = jnp.concatenate([theirs.astype(F32), owns.astype(F32)], axis=0)
    values_a = jnp.concatenate([far_a + rows, pairs[:, 0, :]], axis=0)
    values_b = jnp.concatenate([far_b, offset - shift + rows], axis=0)
    square = (lanes, lanes)
    row = lax.broadcasted_iota(jnp.int32, square, 0)
    col = lax.broadcasted_iota(jnp.int32, square, 1)
    ahead = jnp.where(row < col, 1.0, 0.0).astype(BF16)
    within = dot(cross.astype(BF16), ahead)
    sums = jnp.sum(cross, axis=1, keepdims=True)
    slots = hot_a.shape[0]
    packed = lax.broadcasted_iota(jnp.int32, (slots, lanes), 0).astype(F32)
    lane_rows = lax.broadcasted_iota(jnp.int32, (2 * rows, lanes), 0)
    base = jnp.zeros((1, 1), F32)
    total_a = jnp.zeros(hot_a.shape, F32)
    total_b = jnp.zeros(hot_b.shape, F32)
    bases = []
    for tile in range(2 * tiles):
        bases.append(base)
        place = jnp.where(cross[tile : tile + 1] > 0, within[tile : tile + 1] + base, -1.0)
        select = jnp.where(packed == place, 1.0, 0.0).astype(BF16)
        for values, which in ((values_a, 0), (values_b, 1)):
            ones = jnp.where(lane_rows == values[tile : tile + 1], 1.0, 0.0).astype(BF16)
            part = lax.dot_general(
                select, ones, (((1,), (1,)), ((), ())), preferred_element_type=F32
            )
            if which:
                total_b = total_b + part
            else:
                total_a = total_a + part
        base = base + sums[tile : tile + 1]
    hot_a[...] = total_a.astype(BF16)
    hot_b[...] = total_b.astype(BF16)
    within_columns = columns_of(within)
    cross_columns = columns_of(cross)
    for tile in range(tiles):
        mine = tiles + tile
        live_column = cross_columns[:, mine : mine + 1] > 0
        column = within_columns[:, mine : mine + 1] + bases[mine]
        target = pl.ds(tile * lanes, lanes)
        spread[target, :] = hot_rows(jnp.where(live_column, column, -1.0), spread.shape[1])
        column = jnp.where(live_column, column - bases[tiles], -1.0)
        back[target, :] = hot_rows(column, back.shape[1])
        rest[target, :] = hot_rows(column - back.shape[1], rest.shape[1])
    count_ref[0] = jnp.sum(cross).astype(jnp.int32)


def far_kernel(parts, first, info_ref, count_ref, *refs):
    refs = list(refs)

    def take(number):
        taken = refs[:number]
        del refs[:number]
        return taken

    white = take(parts)
    direct = take(parts)
    across = take(parts) if first else direct
    common_ref, table_ref, mean_ref, hot_a, hot_b, before_ref, acc_ref = take(7)
    sent_ref, rest_ref = (None, None) if first else take(2)
    work_ref, load_sem, store_sem = take(3)
    held = refs
    rows = direct[0].shape[0]
    step = pl.program_id(0)
    last = pl.num_programs(0) - 1
    blocks = (count_ref[0] + FAR_BLOCK - 1) // FAR_BLOCK

    def span(block):
        return pl.ds(pl.multiple_of(block * FAR_BLOCK, FAR_BLOCK), FAR_BLOCK)

    def load(block):
        return pltpu.make_async_copy(
            before_ref.at[span(block), :], work_ref.at[span(block), :], load_sem.at[block]
        )

    def store(block):
        return pltpu.make_async_copy(
            work_ref.at[span(block), :], acc_ref.at[span(block), :], store_sem.at[block]
        )

    if not first:

        @pl.when(step == 0)
        def _():
            lax.fori_loop(0, blocks, lambda block, _: load(block).start(), None)

    for group, w_ref in enumerate(held):
        start = group * GROUP
        for part in range(parts):
            w_ref[pl.ds(0, rows), pl.ds(part * GROUP, GROUP)] = white[part][
                :, pl.ds(start, GROUP)
            ]
        if first:
            pl.when(info_ref[7] == 0)(
                lambda: whiten_into(w_ref, rows, direct, common_ref, mean_ref, start)
            )
            pl.when(info_ref[7] != 0)(
                lambda: whiten_into(w_ref, rows, across, common_ref, mean_ref, start)
            )
        else:
            whiten_into(w_ref, rows, direct, common_ref, mean_ref, start)

    def one_block(block, _):
        target = span(block)
        gained = None
        for group, w_ref in enumerate(held):
            part = correlate_rows(
                hot_a[target, :], hot_b[target, :], w_ref, table_ref, group * GROUP
            )
            gained = part if gained is None else gained + part

        @pl.when(step == 0)
        def _():
            if first:
                work_ref[target, :] = gained
            else:
                load(block).wait()
                work_ref[target, :] += gained

        @pl.when(step > 0)
        def _():
            work_ref[target, :] += gained

        pl.when(step == last)(lambda: store(block).start())

    lax.fori_loop(0, blocks, one_block, None)

    @pl.when(step == last)
    def _():
        lax.fori_loop(0, blocks, lambda block, _: store(block).wait(), None)
        if first:
            return
        sent = sent_ref.shape[0]
        used = lax.broadcasted_iota(jnp.int32, (sent + rest_ref.shape[0], 1), 0)
        used = used < blocks * FAR_BLOCK
        for ref, at in ((sent_ref, 0), (rest_ref, sent)):
            ours = slice(at, at + ref.shape[0])
            ref[...] = jnp.where(used[ours], work_ref[ours, :], 0.0).astype(BF16)


def prepare_kernel(width, counts, info_ref, x_ref, pairs_ref, live_ref, flat_ref, total_ref, code_ref, *sent):
    bins = x_ref.shape[3]
    parts = flat_ref.shape[1] // bins
    flat_ref[...] = x_ref[...].reshape(flat_ref.shape)
    total = x_ref[0].astype(F32)
    for row in range(1, x_ref.shape[0]):
        total = total + x_ref[row].astype(F32)

    @pl.when(pl.program_id(0) == 0)
    def _():
        total_ref[:, :, pl.ds(0, bins)] = total
        pairs = pairs_ref[...]
        live = live_ref[...]
        listed = [pairs[:, 0, :] - info_ref[3], pairs[:, 1, :] - pairs[:, 0, :], live]
        spare = code_ref.shape[0] - 3 * live.shape[0]
        if spare:
            listed.append(jnp.zeros((spare, live.shape[1]), jnp.int32))
        code_ref[...] = jnp.concatenate(listed, axis=0).astype(F32).astype(BF16)
        second = pairs[:, 1, :] - info_ref[1]
        crossing = (second >= 0) & (second < info_ref[2]) & (live_ref[...] != 0)
        number = jnp.sum(jnp.where(crossing, 1.0, 0.0))
        flag = jnp.where(number > BACK_ROWS, 1.0, 0.0)
        lanes = total_ref.shape[2] - bins
        total_ref[:, :, pl.ds(bins, lanes)] = jnp.full(total_ref.shape[:2] + (lanes,), flag, F32)

    @pl.when(pl.program_id(0) > 0)
    def _():
        total_ref[:, :, pl.ds(0, bins)] += total

    done = 0
    for pieces, ref in zip(counts, sent):
        for part in range(parts):
            start = part * bins + done * width + info_ref[0]
            ref[:, pl.ds(part * pieces * width, pieces * width)] = flat_ref[
                :, pl.ds(pl.multiple_of(start, width), pieces * width)
            ]
        done += pieces


def gather_kernel(scale, count_ref, near_ref, spread_ref, far_ref, o_ref, held, sem):
    blocks = (count_ref[0] + FAR_BLOCK - 1) // FAR_BLOCK

    def load(block):
        rows = pl.ds(pl.multiple_of(block * FAR_BLOCK, FAR_BLOCK), FAR_BLOCK)
        return pltpu.make_async_copy(far_ref.at[rows, :], held.at[rows, :], sem.at[block])

    lax.fori_loop(0, blocks, lambda block, _: load(block).start(), None)
    o_ref[...] = near_ref[...] * scale

    def add(block, _):
        load(block).wait()
        start = pl.multiple_of(block * FAR_BLOCK, FAR_BLOCK)
        far = held[pl.ds(start, FAR_BLOCK), :] * scale
        high = far.astype(BF16)
        low = (far - high.astype(F32)).astype(BF16)
        spread = spread_ref[:, pl.ds(start, FAR_BLOCK)]
        o_ref[...] += dot(spread, high) + dot(spread, low)

    lax.fori_loop(0, blocks, add, None)


def merge_kernel(scale, mine_ref, *refs):
    total = mine_ref[...]
    for spread_ref, back_ref in zip(refs[0:-1:2], refs[1:-1:2]):
        total = total + dot(spread_ref[...], back_ref[...]) * scale
    refs[-1][...] = total


def params(mebibytes=56):
    return dict(
        compiler_params=pltpu.CompilerParams(vmem_limit_bytes=mebibytes * 1024 * 1024),
        cost_estimate=pl.CostEstimate(flops=1000, bytes_accessed=1000, transcendentals=0),
    )


def whole(shape):
    return pl.BlockSpec(shape, lambda *_: (0,) * len(shape))


def prepare(spectra, info, width, counts, pairs, live):
    rows, windows, two, bins = spectra.shape
    parts = windows * two
    code_rows = -(-3 * live.shape[0] // 16) * 16
    lanes = [parts * bins] + [parts * pieces * width for pieces in counts]
    blocks = [pl.BlockSpec((ROW_BLOCK, n), lambda i, s: (i, 0)) for n in lanes]
    shapes = [jax.ShapeDtypeStruct((rows, n), BF16) for n in lanes]
    return pl.pallas_call(
        functools.partial(prepare_kernel, width, counts),
        grid_spec=pltpu.PrefetchScalarGridSpec(
            num_scalar_prefetch=1,
            grid=(rows // ROW_BLOCK,),
            in_specs=[
                pl.BlockSpec((ROW_BLOCK, windows, two, bins), lambda i, s: (i, 0, 0, 0)),
                whole(pairs.shape),
                whole(live.shape),
            ],
            out_specs=blocks[:1]
            + [whole((windows, two, bins + live.shape[1])), whole((code_rows, live.shape[1]))]
            + blocks[1:],
        ),
        out_shape=shapes[:1] + [jax.ShapeDtypeStruct((windows, two, bins + live.shape[1]), F32)]
        + [jax.ShapeDtypeStruct((code_rows, live.shape[1]), BF16)]
        + shapes[1:],
        name="prepare",
        **params(),
    )(info, spectra, pairs, live)


def behind(array, *after):
    anywhere = pl.BlockSpec(memory_space=pl.ANY)
    return pl.pallas_call(
        lambda *refs: None,
        in_specs=[anywhere] * (1 + len(after)),
        out_specs=anywhere,
        out_shape=jax.ShapeDtypeStruct(array.shape, array.dtype),
        input_output_aliases={0: 0},
        name="behind",
        **params(),
    )(array, *after)


def body(spectra, pair_channels, pair_live):
    rows, windows, _, bins = spectra.shape
    parts = 2 * windows
    count = lax.axis_size("row")
    me = lax.axis_index("row")
    odd = me % 2
    first_row = me * rows
    half = bins // 2
    fast = [(i, i ^ 1) for i in range(count)]

    def slow_of(*places):
        up = [(i, i + 1) for i in range(1, count - 1, 2) if i % 4 in places]
        return up + [(b, a) for a, b in up]

    slow = slow_of(1, 3)
    piece = half // 4
    send_start = (1 - odd) * half

    tiles, tile = pair_live.shape
    slots = tiles * tile
    counts = (2, 2)
    wide = NEAR_GROUPS * GROUP
    near_shift = jnp.where(odd == 1, -rows, rows)
    across = (((me + 1) // 2) % 2 == 0).astype(jnp.int32)
    pairs = jnp.swapaxes(pair_channels, 1, 2)
    far_low = first_row + jnp.where(odd == 1, rows, -rows)
    facts = jnp.stack(
        [
            send_start,
            far_low,
            jnp.int32(rows),
            first_row,
            near_shift,
            odd * (half // wide),
            odd * (half // piece),
            across,
        ]
    )
    flat, total, code, *chunks = prepare(
        spectra,
        facts,
        piece,
        counts,
        pairs,
        pair_live,
    )
    far_code = lax.ppermute(code, "row", slow)
    if count & (count - 1):
        far_direct = lax.ppermute(chunks[0], "row", slow_of(1))
        round_one = total
        reach = lax.psum(total, "row")
        partner_rows = lax.ppermute(flat, "row", fast)
    else:
        reach = total
        jump = 1
        while jump < count:
            others = [
                lax.ppermute(reach, "row", [(i, i ^ k) for i in range(count)])
                for k in (jump, 2 * jump, 3 * jump)
                if 2 * jump < count or k == jump
            ]
            reach = functools.reduce(jnp.add, others, reach)
            if jump == 1:
                reach = round_one = behind(reach, far_code)
                far_direct = lax.ppermute(behind(chunks[0], reach), "row", slow_of(1))
                flat = behind(flat, reach)
                partner_rows = lax.ppermute(flat, "row", fast)
            jump *= 4
    common = reach / (rows * count)
    far_across = lax.ppermute(behind(chunks[0], reach), "row", slow_of(3))
    far_second = lax.ppermute(behind(chunks[1], reach), "row", slow)

    lists = (pairs, pair_live)
    list_specs = [whole(pairs.shape), whole(pair_live.shape)]
    hot_a, hot_b, spread, back_spread, rest_spread, cross_count = pl.pallas_call(
        plan_kernel,
        grid_spec=pltpu.PrefetchScalarGridSpec(
            num_scalar_prefetch=1,
            grid=(1,),
            in_specs=list_specs
            + [whole(code.shape)]
            + [pl.BlockSpec(memory_space=pl.ANY)],
            out_specs=[
                whole((2 * slots, 2 * rows)),
                whole((2 * slots, 2 * rows)),
                whole((slots, 2 * slots)),
                whole((slots, BACK_ROWS)),
                whole((slots, slots - BACK_ROWS)),
                pl.BlockSpec(memory_space=pltpu.SMEM),
            ],
        ),
        out_shape=[
            jax.ShapeDtypeStruct((2 * slots, 2 * rows), BF16),
            jax.ShapeDtypeStruct((2 * slots, 2 * rows), BF16),
            jax.ShapeDtypeStruct((slots, 2 * slots), BF16),
            jax.ShapeDtypeStruct((slots, BACK_ROWS), BF16),
            jax.ShapeDtypeStruct((slots, slots - BACK_ROWS), BF16),
            jax.ShapeDtypeStruct((1,), jnp.int32),
        ],
        name="plan",
        **params(),
    )(facts, *lists, far_code, round_one)

    table = jnp.asarray(lag_table(bins, LAGS))
    mean = jnp.asarray(band_mean())

    steps = bins // wide

    def near_call():
        def bin_block(j, s):
            return lax.rem(s[5] + j, steps)

        return pl.pallas_call(
            functools.partial(near_kernel, parts),
            grid_spec=pltpu.PrefetchScalarGridSpec(
                num_scalar_prefetch=1,
                grid=(steps,),
                in_specs=[
                    pl.BlockSpec(
                        (rows, wide),
                        functools.partial(lambda p, j, s: (0, p * steps + bin_block(j, s)), p),
                    )
                    for _ in range(2)
                    for p in range(parts)
                ]
                + [
                    pl.BlockSpec((windows, 2, wide), lambda j, s: (0, 0, bin_block(j, s))),
                    pl.BlockSpec((2, wide, LAGS), lambda j, s: (0, bin_block(j, s), 0)),
                    whole((GROUP, GROUP)),
                ]
                + list_specs
                + [
                    pl.BlockSpec((windows, 2, tile), lambda j, s: (0, 0, bins // tile)),
                    pl.BlockSpec(memory_space=pl.ANY),
                ],
                out_specs=[whole((slots, LAGS))]
                + [pl.BlockSpec((rows, wide), lambda j, s: (0, j))] * parts
                + [pl.BlockSpec(memory_space=pltpu.SMEM)],
                scratch_shapes=[pltpu.VMEM((slots, 2 * rows), BF16)] * 2
                + [pltpu.VMEM((2 * rows, parts * GROUP), BF16)] * NEAR_GROUPS,
            ),
            out_shape=[jax.ShapeDtypeStruct((slots, LAGS), F32)]
            + [jax.ShapeDtypeStruct((rows, bins), BF16)] * parts
            + [jax.ShapeDtypeStruct((2,), jnp.int32)],
            name="near_pairs",
            **params(60),
        )(
            facts,
            *[flat] * parts,
            *[partner_rows] * parts,
            common,
            table,
            mean,
            *lists,
            common,
            cross_count,
        )

    near_acc, *white, exceeds = near_call()


    def far_call(first, arrays, before):
        pieces = half // piece // 2
        base = 0 if first else pieces
        choose = (lambda s, k: s[7] == k) if first else (lambda s, k: True)
        back_rows = () if first else (BACK_ROWS, slots - BACK_ROWS)
        return pl.pallas_call(
            functools.partial(far_kernel, parts, first),
            grid_spec=pltpu.PrefetchScalarGridSpec(
                num_scalar_prefetch=2,
                grid=(pieces,),
                in_specs=[
                    pl.BlockSpec((rows, piece), lambda j, s, n: (0, base + j)) for _ in range(parts)
                ]
                + [
                    pl.BlockSpec(
                        (rows, piece),
                        functools.partial(
                            lambda k, p, j, s, n: (0, jnp.where(choose(s, k), p * pieces + j, 0)),
                            k,
                            p,
                        ),
                    )
                    for k in range(len(arrays))
                    for p in range(parts)
                ]
                + [
                    pl.BlockSpec((windows, 2, piece), lambda j, s, n: (0, 0, s[6] + base + j)),
                    pl.BlockSpec((2, piece, LAGS), lambda j, s, n: (0, s[6] + base + j, 0)),
                    whole((GROUP, GROUP)),
                    whole((2 * slots, 2 * rows)),
                    whole((2 * slots, 2 * rows)),
                    pl.BlockSpec(memory_space=pl.ANY),
                ],
                out_specs=[pl.BlockSpec(memory_space=pl.ANY)]
                + [whole((n, LAGS)) for n in back_rows],
                scratch_shapes=[
                    pltpu.VMEM((2 * slots, LAGS), F32),
                    pltpu.SemaphoreType.DMA((2 * slots // FAR_BLOCK,)),
                    pltpu.SemaphoreType.DMA((2 * slots // FAR_BLOCK,)),
                ]
                + [pltpu.VMEM((2 * rows, parts * GROUP), BF16)] * (piece // GROUP),
            ),
            out_shape=[jax.ShapeDtypeStruct((2 * slots, LAGS), F32)]
            + [jax.ShapeDtypeStruct((n, LAGS), BF16) for n in back_rows],
            name="far_pairs",
            **params(),
        )(
            facts,
            cross_count,
            *white,
            *[a for a in arrays for _ in range(parts)],
            common,
            table,
            mean,
            hot_a,
            hot_b,
            before,
        )

    (before,) = far_call(True, (far_direct, far_across), near_acc)
    far_acc, theirs, their_rest = far_call(False, (far_second,), before)

    scale = 1.0 / math.sqrt(bins * windows)
    back = lax.ppermute(theirs, "row", slow)
    gathered = pl.pallas_call(
        functools.partial(gather_kernel, scale),
        grid_spec=pltpu.PrefetchScalarGridSpec(
            num_scalar_prefetch=1,
            grid=(1,),
            in_specs=[
                whole((slots, LAGS)),
                whole((slots, 2 * slots)),
                pl.BlockSpec(memory_space=pl.ANY),
            ],
            out_specs=whole((slots, LAGS)),
            scratch_shapes=[
                pltpu.VMEM((2 * slots, LAGS), F32),
                pltpu.SemaphoreType.DMA((2 * slots // FAR_BLOCK,)),
            ],
        ),
        out_shape=jax.ShapeDtypeStruct((slots, LAGS), F32),
        name="gather",
        **params(),
    )(cross_count, near_acc, spread, far_acc)

    def merge(*spread_back):
        return pl.pallas_call(
            functools.partial(merge_kernel, scale),
            grid=(tiles,),
            in_specs=[pl.BlockSpec((tile, LAGS), lambda i: (i, 0))]
            + [
                spec
                for k in range(0, len(spread_back), 2)
                for spec in (
                    pl.BlockSpec((tile, spread_back[k].shape[1]), lambda i: (i, 0)),
                    whole(spread_back[k + 1].shape),
                )
            ],
            out_specs=pl.BlockSpec((tile, LAGS), lambda i: (i, 0)),
            out_shape=jax.ShapeDtypeStruct((slots, LAGS), F32),
            name="merge",
            **params(),
        )(gathered, *spread_back)

    result = lax.cond(
        exceeds[0] > 0,
        lambda: merge(back_spread, back, rest_spread, lax.ppermute(their_rest, "row", slow)),
        lambda: merge(back_spread, back),
    )
    return result.reshape(pair_live.shape + (LAGS,))


def solution(mesh):
    placed = (P(("day", "row"), None, None, None), P("row", None, None), P("row", None))
    return jax.shard_map(
        body, mesh=mesh, in_specs=placed, out_specs=P(("day", "row"), None, None), check_vma=False
    )
```

```python
import functools
import math

import jax
import jax.numpy as jnp
import numpy as np
from jax import lax
from jax.experimental import pallas as pl
from jax.experimental.pallas import tpu as pltpu
from jax.sharding import PartitionSpec as P

BAND = 64
LAGS = 512
GROUP = 256
NEAR_GROUPS = 4
FAR_BLOCK = 256
BACK_ROWS = 160
ROW_BLOCK = 32
TINY = 1e-37
F32 = jnp.float32
BF16 = jnp.bfloat16


def lag_table(bins, lags):
    shifts = np.arange(lags, dtype=np.int64)[None, :] - lags // 2
    phase = np.mod(np.arange(bins, dtype=np.int64)[:, None] * shifts, 2 * bins)
    angle = (phase.astype(np.float32) * np.float32(math.pi / bins)).astype(np.float64)
    both = np.stack([np.cos(angle), -np.sin(angle)]).astype(np.float32)
    return both.astype(jnp.bfloat16)


def band_mean():
    rows = np.arange(GROUP)[:, None] // BAND
    cols = np.arange(GROUP)[None, :] // BAND
    return np.where(rows == cols, 1.0 / BAND, 0.0).astype(jnp.bfloat16)


def dot(a, b):
    return jnp.dot(a, b, preferred_element_type=F32)


def whiten_into(w_ref, row0, raws, common_ref, mean_ref, start):
    rows = raws[0].shape[0]
    target = pl.ds(row0, rows)
    cols = pl.ds(start, GROUP)
    for w in range(len(raws) // 2):
        re = raws[2 * w][:, cols].astype(F32) - common_ref[w, 0:1, cols]
        im = raws[2 * w + 1][:, cols].astype(F32) - common_ref[w, 1:2, cols]
        power = re * re + im * im
        magnitude = (power * lax.rsqrt(jnp.maximum(power, TINY))).astype(BF16)
        scale = 1.0 / (dot(magnitude, mean_ref[...]) + 1e-06)
        w_ref[target, pl.ds(2 * w * GROUP, GROUP)] = (re * scale).astype(BF16)
        w_ref[target, pl.ds((2 * w + 1) * GROUP, GROUP)] = (im * scale).astype(BF16)


def columns_of(rows_of_tiles):
    lanes = rows_of_tiles.shape[1]
    padded = rows_of_tiles.astype(F32)
    if missing := -padded.shape[0] % 8:
        padded = jnp.concatenate([padded, jnp.zeros((missing, lanes), F32)], axis=0)
    square = (lanes, lanes)
    same = lax.broadcasted_iota(jnp.int32, square, 0) == lax.broadcasted_iota(jnp.int32, square, 1)
    unit = jnp.where(same, 1.0, 0.0).astype(BF16)
    return lax.dot_general(
        unit, padded.astype(BF16), (((1,), (1,)), ((), ())), preferred_element_type=F32
    )


def hot_rows(column, width):
    lane = lax.broadcasted_iota(jnp.int32, (column.shape[0], width), 1).astype(F32)
    return jnp.where(column == lane, 1.0, 0.0).astype(BF16)


def fill_hot(values, hot_ref):
    tiles, lanes = values.shape
    columns = columns_of(values)
    for tile in range(tiles):
        hot_ref[pl.ds(tile * lanes, lanes), :] = hot_rows(
            columns[:, tile : tile + 1], hot_ref.shape[1]
        )


def correlate_rows(hot_a, hot_b, w_ref, table_ref, start):
    both = dot(jnp.concatenate([hot_a, hot_b], axis=0), w_ref[...])
    a, b = both[: hot_a.shape[0]], both[hot_a.shape[0] :]
    real = imag = None
    for w in range(w_ref.shape[1] // (2 * GROUP)):
        ar, ai, br, bi = (
            x[:, (2 * w + r) * GROUP : (2 * w + r + 1) * GROUP] for x in (a, b) for r in range(2)
        )
        re = ar * br + ai * bi
        im = ai * br - ar * bi
        real = re if real is None else real + re
        imag = im if imag is None else imag + im
    rows = pl.ds(start, GROUP)
    return dot(real.astype(BF16), table_ref[0, rows, :]) + dot(
        imag.astype(BF16), table_ref[1, rows, :]
    )


def near_kernel(parts, info_ref, *refs):
    refs = list(refs)

    def take(number):
        taken = refs[:number]
        del refs[:number]
        return taken

    own, other = take(parts), take(parts)
    common_ref, table_ref, mean_ref, pairs_ref, live_ref, flag_ref, _ = take(7)
    (acc_ref,) = take(1)
    white = take(parts)
    (exceeds_ref,) = take(1)
    hot_a, hot_b, *held = refs
    rows = own[0].shape[0]

    @pl.when(pl.program_id(0) == 0)
    def _():
        acc_ref[...] = jnp.zeros_like(acc_ref)
        exceeds_ref[0] = (jnp.max(flag_ref[...]) > 0).astype(jnp.int32)
        lists = live_ref.shape
        order = lax.broadcasted_iota(jnp.int32, lists, 0) * lists[1]
        order = (order + lax.broadcasted_iota(jnp.int32, lists, 1) + 1).astype(F32)
        exceeds_ref[1] = jnp.max(jnp.where(live_ref[...] != 0, order, 0.0)).astype(jnp.int32)
        shift = info_ref[4]
        pairs = pairs_ref[...] - info_ref[3]
        offset = pairs[:, 1, :]
        live = live_ref[...] != 0
        inside = (offset >= 0) & (offset < rows)
        beside = (offset >= shift) & (offset < shift + rows)
        place = jnp.where(inside, offset, jnp.where(beside, offset - shift + rows, -1))
        fill_hot(jnp.where(live, pairs[:, 0, :], -1), hot_a)
        fill_hot(jnp.where(live, place, -1), hot_b)

    def prepare(group):
        start = group * GROUP
        w_ref = held[group]
        whiten_into(w_ref, 0, own, common_ref, mean_ref, start)
        whiten_into(w_ref, rows, other, common_ref, mean_ref, start)
        for part in range(len(white)):
            white[part][:, pl.ds(start, GROUP)] = w_ref[
                pl.ds(0, rows), pl.ds(part * GROUP, GROUP)
            ]

    def run(block):
        slots = pl.ds(0, block)
        prepare(0)
        for group in range(len(held)):
            if group + 1 < len(held):
                prepare(group + 1)
            acc_ref[slots, :] += correlate_rows(
                hot_a[slots, :], hot_b[slots, :], held[group], table_ref, group * GROUP
            )

    total = hot_a.shape[0]
    pl.when(exceeds_ref[1] <= total // 2)(lambda: run(total // 2))
    pl.when(exceeds_ref[1] > total // 2)(lambda: run(total))


def plan_kernel(info_ref, pairs_ref, live_ref, code_ref, _, hot_a, hot_b, spread, back, rest, count_ref):
    tiles, lanes = live_ref.shape
    rows = hot_a.shape[1] // 2
    shift = -info_ref[4]
    pairs = pairs_ref[...] - info_ref[3]
    code = code_ref[...].astype(F32).astype(jnp.int32)
    far_a = code[0:tiles]
    far_b = far_a + code[tiles : 2 * tiles] + shift
    theirs = (far_b >= 0) & (far_b < rows) & (code[2 * tiles : 3 * tiles] != 0)
    offset = pairs[:, 1, :]
    owns = (offset >= shift) & (offset < shift + rows) & (live_ref[...] != 0)
    cross = jnp.concatenate([theirs.astype(F32), owns.astype(F32)], axis=0)
    values_a = jnp.concatenate([far_a + rows, pairs[:, 0, :]], axis=0)
    values_b = jnp.concatenate([far_b, offset - shift + rows], axis=0)
    square = (lanes, lanes)
    row = lax.broadcasted_iota(jnp.int32, square, 0)
    col = lax.broadcasted_iota(jnp.int32, square, 1)
    ahead = jnp.where(row < col, 1.0, 0.0).astype(BF16)
    within = dot(cross.astype(BF16), ahead)
    sums = jnp.sum(cross, axis=1, keepdims=True)
    slots = hot_a.shape[0]
    packed = lax.broadcasted_iota(jnp.int32, (slots, lanes), 0).astype(F32)
    lane_rows = lax.broadcasted_iota(jnp.int32, (2 * rows, lanes), 0)
    base = jnp.zeros((1, 1), F32)
    total_a = jnp.zeros(hot_a.shape, F32)
    total_b = jnp.zeros(hot_b.shape, F32)
    bases = []
    for tile in range(2 * tiles):
        bases.append(base)
        place = jnp.where(cross[tile : tile + 1] > 0, within[tile : tile + 1] + base, -1.0)
        select = jnp.where(packed == place, 1.0, 0.0).astype(BF16)
        for values, which in ((values_a, 0), (values_b, 1)):
            ones = jnp.where(lane_rows == values[tile : tile + 1], 1.0, 0.0).astype(BF16)
            part = lax.dot_general(
                select, ones, (((1,), (1,)), ((), ())), preferred_element_type=F32
            )
            if which:
                total_b = total_b + part
            else:
                total_a = total_a + part
        base = base + sums[tile : tile + 1]
    hot_a[...] = total_a.astype(BF16)
    hot_b[...] = total_b.astype(BF16)
    within_columns = columns_of(within)
    cross_columns = columns_of(cross)
    for tile in range(tiles):
        mine = tiles + tile
        live_column = cross_columns[:, mine : mine + 1] > 0
        column = within_columns[:, mine : mine + 1] + bases[mine]
        target = pl.ds(tile * lanes, lanes)
        spread[target, :] = hot_rows(jnp.where(live_column, column, -1.0), spread.shape[1])
        column = jnp.where(live_column, column - bases[tiles], -1.0)
        back[target, :] = hot_rows(column, back.shape[1])
        rest[target, :] = hot_rows(column - back.shape[1], rest.shape[1])
    count_ref[0] = jnp.sum(cross).astype(jnp.int32)


def far_kernel(parts, first, info_ref, count_ref, *refs):
    refs = list(refs)

    def take(number):
        taken = refs[:number]
        del refs[:number]
        return taken

    white = take(parts)
    direct = take(parts)
    across = take(parts) if first else direct
    common_ref, table_ref, mean_ref, hot_a, hot_b, before_ref, acc_ref = take(7)
    sent_ref, rest_ref = (None, None) if first else take(2)
    work_ref, load_sem, store_sem = take(3)
    held = refs
    rows = direct[0].shape[0]
    step = pl.program_id(0)
    last = pl.num_programs(0) - 1
    blocks = (count_ref[0] + FAR_BLOCK - 1) // FAR_BLOCK

    def span(block):
        return pl.ds(pl.multiple_of(block * FAR_BLOCK, FAR_BLOCK), FAR_BLOCK)

    def load(block):
        return pltpu.make_async_copy(
            before_ref.at[span(block), :], work_ref.at[span(block), :], load_sem.at[block]
        )

    def store(block):
        return pltpu.make_async_copy(
            work_ref.at[span(block), :], acc_ref.at[span(block), :], store_sem.at[block]
        )

    if not first:

        @pl.when(step == 0)
        def _():
            lax.fori_loop(0, blocks, lambda block, _: load(block).start(), None)

    for group, w_ref in enumerate(held):
        start = group * GROUP
        for part in range(parts):
            w_ref[pl.ds(0, rows), pl.ds(part * GROUP, GROUP)] = white[part][
                :, pl.ds(start, GROUP)
            ]
        if first:
            pl.when(info_ref[7] == 0)(
                lambda: whiten_into(w_ref, rows, direct, common_ref, mean_ref, start)
            )
            pl.when(info_ref[7] != 0)(
                lambda: whiten_into(w_ref, rows, across, common_ref, mean_ref, start)
            )
        else:
            whiten_into(w_ref, rows, direct, common_ref, mean_ref, start)

    def one_block(block, _):
        target = span(block)
        gained = None
        for group, w_ref in enumerate(held):
            part = correlate_rows(
                hot_a[target, :], hot_b[target, :], w_ref, table_ref, group * GROUP
            )
            gained = part if gained is None else gained + part

        @pl.when(step == 0)
        def _():
            if first:
                work_ref[target, :] = gained
            else:
                load(block).wait()
                work_ref[target, :] += gained

        @pl.when(step > 0)
        def _():
            work_ref[target, :] += gained

        pl.when(step == last)(lambda: store(block).start())

    lax.fori_loop(0, blocks, one_block, None)

    @pl.when(step == last)
    def _():
        lax.fori_loop(0, blocks, lambda block, _: store(block).wait(), None)
        if first:
            return
        sent = sent_ref.shape[0]
        used = lax.broadcasted_iota(jnp.int32, (sent + rest_ref.shape[0], 1), 0)
        used = used < blocks * FAR_BLOCK
        for ref, at in ((sent_ref, 0), (rest_ref, sent)):
            ours = slice(at, at + ref.shape[0])
            ref[...] = jnp.where(used[ours], work_ref[ours, :], 0.0).astype(BF16)


def prepare_kernel(width, counts, info_ref, x_ref, pairs_ref, live_ref, flat_ref, total_ref, code_ref, *sent):
    bins = x_ref.shape[3]
    parts = flat_ref.shape[1] // bins
    flat_ref[...] = x_ref[...].reshape(flat_ref.shape)
    total = x_ref[0].astype(F32)
    for row in range(1, x_ref.shape[0]):
        total = total + x_ref[row].astype(F32)

    @pl.when(pl.program_id(0) == 0)
    def _():
        total_ref[:, :, pl.ds(0, bins)] = total
        pairs = pairs_ref[...]
        live = live_ref[...]
        listed = [pairs[:, 0, :] - info_ref[3], pairs[:, 1, :] - pairs[:, 0, :], live]
        spare = code_ref.shape[0] - 3 * live.shape[0]
        if spare:
            listed.append(jnp.zeros((spare, live.shape[1]), jnp.int32))
        code_ref[...] = jnp.concatenate(listed, axis=0).astype(F32).astype(BF16)
        second = pairs[:, 1, :] - info_ref[1]
        crossing = (second >= 0) & (second < info_ref[2]) & (live_ref[...] != 0)
        number = jnp.sum(jnp.where(crossing, 1.0, 0.0))
        flag = jnp.where(number > BACK_ROWS, 1.0, 0.0)
        lanes = total_ref.shape[2] - bins
        total_ref[:, :, pl.ds(bins, lanes)] = jnp.full(total_ref.shape[:2] + (lanes,), flag, F32)

    @pl.when(pl.program_id(0) > 0)
    def _():
        total_ref[:, :, pl.ds(0, bins)] += total

    done = 0
    for pieces, ref in zip(counts, sent[1:]):
        for part in range(parts):
            start = part * bins + done * width + info_ref[0]
            ref[:, pl.ds(part * pieces * width, pieces * width)] = flat_ref[
                :, pl.ds(pl.multiple_of(start, width), pieces * width)
            ]
        done += pieces
    sent[0][...] = sent[1][...]


def gather_kernel(scale, count_ref, near_ref, spread_ref, far_ref, o_ref, held, sem):
    blocks = (count_ref[0] + FAR_BLOCK - 1) // FAR_BLOCK

    def load(block):
        rows = pl.ds(pl.multiple_of(block * FAR_BLOCK, FAR_BLOCK), FAR_BLOCK)
        return pltpu.make_async_copy(far_ref.at[rows, :], held.at[rows, :], sem.at[block])

    lax.fori_loop(0, blocks, lambda block, _: load(block).start(), None)
    o_ref[...] = near_ref[...] * scale

    def add(block, _):
        load(block).wait()
        start = pl.multiple_of(block * FAR_BLOCK, FAR_BLOCK)
        far = held[pl.ds(start, FAR_BLOCK), :] * scale
        high = far.astype(BF16)
        low = (far - high.astype(F32)).astype(BF16)
        spread = spread_ref[:, pl.ds(start, FAR_BLOCK)]
        o_ref[...] += dot(spread, high) + dot(spread, low)

    lax.fori_loop(0, blocks, add, None)


def merge_kernel(scale, mine_ref, *refs):
    total = mine_ref[...]
    for spread_ref, back_ref in zip(refs[0:-1:2], refs[1:-1:2]):
        total = total + dot(spread_ref[...], back_ref[...]) * scale
    refs[-1][...] = total


def params(mebibytes=56):
    return dict(
        compiler_params=pltpu.CompilerParams(vmem_limit_bytes=mebibytes * 1024 * 1024),
        cost_estimate=pl.CostEstimate(flops=1000, bytes_accessed=1000, transcendentals=0),
    )


def whole(shape):
    return pl.BlockSpec(shape, lambda *_: (0,) * len(shape))


def prepare(spectra, info, width, counts, pairs, live):
    rows, windows, two, bins = spectra.shape
    parts = windows * two
    code_rows = -(-3 * live.shape[0] // 16) * 16
    lanes = [parts * bins] + [parts * pieces * width for pieces in counts[:1] + counts]
    blocks = [pl.BlockSpec((ROW_BLOCK, n), lambda i, s: (i, 0)) for n in lanes]
    shapes = [jax.ShapeDtypeStruct((rows, n), BF16) for n in lanes]
    return pl.pallas_call(
        functools.partial(prepare_kernel, width, counts),
        grid_spec=pltpu.PrefetchScalarGridSpec(
            num_scalar_prefetch=1,
            grid=(rows // ROW_BLOCK,),
            in_specs=[
                pl.BlockSpec((ROW_BLOCK, windows, two, bins), lambda i, s: (i, 0, 0, 0)),
                whole(pairs.shape),
                whole(live.shape),
            ],
            out_specs=blocks[:1]
            + [whole((windows, two, bins + live.shape[1])), whole((code_rows, live.shape[1]))]
            + blocks[1:],
        ),
        out_shape=shapes[:1] + [jax.ShapeDtypeStruct((windows, two, bins + live.shape[1]), F32)]
        + [jax.ShapeDtypeStruct((code_rows, live.shape[1]), BF16)]
        + shapes[1:],
        name="prepare",
        **params(),
    )(info, spectra, pairs, live)


def behind(array, *after):
    anywhere = pl.BlockSpec(memory_space=pl.ANY)
    return pl.pallas_call(
        lambda *refs: None,
        in_specs=[anywhere] * (1 + len(after)),
        out_specs=anywhere,
        out_shape=jax.ShapeDtypeStruct(array.shape, array.dtype),
        input_output_aliases={0: 0},
        name="behind",
        **params(),
    )(array, *after)


def body(spectra, pair_channels, pair_live):
    rows, windows, _, bins = spectra.shape
    parts = 2 * windows
    count = lax.axis_size("row")
    me = lax.axis_index("row")
    odd = me % 2
    first_row = me * rows
    half = bins // 2
    fast = [(i, i ^ 1) for i in range(count)]

    def slow_of(*places):
        up = [(i, i + 1) for i in range(1, count - 1, 2) if i % 4 in places]
        return up + [(b, a) for a, b in up]

    slow = slow_of(1, 3)
    piece = half // 4
    send_start = (1 - odd) * half

    tiles, tile = pair_live.shape
    slots = tiles * tile
    counts = (2, 2)
    wide = NEAR_GROUPS * GROUP
    near_shift = jnp.where(odd == 1, -rows, rows)
    across = (((me + 1) // 2) % 2 == 0).astype(jnp.int32)
    pairs = jnp.swapaxes(pair_channels, 1, 2)
    far_low = first_row + jnp.where(odd == 1, rows, -rows)
    facts = jnp.stack(
        [
            send_start,
            far_low,
            jnp.int32(rows),
            first_row,
            near_shift,
            odd * (half // wide),
            odd * (half // piece),
            across,
        ]
    )
    flat, total, code, *chunks = prepare(
        spectra,
        facts,
        piece,
        counts,
        pairs,
        pair_live,
    )
    far_code = lax.ppermute(code, "row", slow)
    if count & (count - 1):
        far_direct = lax.ppermute(chunks[0], "row", slow_of(1))
        round_one = total
        reach = lax.psum(total, "row")
        partner_rows = lax.ppermute(flat, "row", fast)
    else:
        reach = total
        jump = 1
        while jump < count:
            others = [
                lax.ppermute(reach, "row", [(i, i ^ k) for i in range(count)])
                for k in (jump, 2 * jump, 3 * jump)
                if 2 * jump < count or k == jump
            ]
            reach = functools.reduce(jnp.add, others, reach)
            if jump == 1:
                reach = round_one = behind(reach, far_code)
                far_direct = lax.ppermute(behind(chunks[0], reach), "row", slow_of(1))
                flat = behind(flat, reach)
                partner_rows = lax.ppermute(flat, "row", fast)
            jump *= 4
    common = reach / (rows * count)
    far_across = lax.ppermute(behind(chunks[1], reach), "row", slow_of(3))
    far_second = lax.ppermute(behind(chunks[2], reach), "row", slow)

    lists = (pairs, pair_live)
    list_specs = [whole(pairs.shape), whole(pair_live.shape)]
    hot_a, hot_b, spread, back_spread, rest_spread, cross_count = pl.pallas_call(
        plan_kernel,
        grid_spec=pltpu.PrefetchScalarGridSpec(
            num_scalar_prefetch=1,
            grid=(1,),
            in_specs=list_specs
            + [whole(code.shape)]
            + [pl.BlockSpec(memory_space=pl.ANY)],
            out_specs=[
                whole((2 * slots, 2 * rows)),
                whole((2 * slots, 2 * rows)),
                whole((slots, 2 * slots)),
                whole((slots, BACK_ROWS)),
                whole((slots, slots - BACK_ROWS)),
                pl.BlockSpec(memory_space=pltpu.SMEM),
            ],
        ),
        out_shape=[
            jax.ShapeDtypeStruct((2 * slots, 2 * rows), BF16),
            jax.ShapeDtypeStruct((2 * slots, 2 * rows), BF16),
            jax.ShapeDtypeStruct((slots, 2 * slots), BF16),
            jax.ShapeDtypeStruct((slots, BACK_ROWS), BF16),
            jax.ShapeDtypeStruct((slots, slots - BACK_ROWS), BF16),
            jax.ShapeDtypeStruct((1,), jnp.int32),
        ],
        name="plan",
        **params(),
    )(facts, *lists, far_code, round_one)

    table = jnp.asarray(lag_table(bins, LAGS))
    mean = jnp.asarray(band_mean())

    steps = bins // wide

    def near_call():
        def bin_block(j, s):
            return lax.rem(s[5] + j, steps)

        return pl.pallas_call(
            functools.partial(near_kernel, parts),
            grid_spec=pltpu.PrefetchScalarGridSpec(
                num_scalar_prefetch=1,
                grid=(steps,),
                in_specs=[
                    pl.BlockSpec(
                        (rows, wide),
                        functools.partial(lambda p, j, s: (0, p * steps + bin_block(j, s)), p),
                    )
                    for _ in range(2)
                    for p in range(parts)
                ]
                + [
                    pl.BlockSpec((windows, 2, wide), lambda j, s: (0, 0, bin_block(j, s))),
                    pl.BlockSpec((2, wide, LAGS), lambda j, s: (0, bin_block(j, s), 0)),
                    whole((GROUP, GROUP)),
                ]
                + list_specs
                + [
                    pl.BlockSpec((windows, 2, tile), lambda j, s: (0, 0, bins // tile)),
                    pl.BlockSpec(memory_space=pl.ANY),
                ],
                out_specs=[whole((slots, LAGS))]
                + [pl.BlockSpec((rows, wide), lambda j, s: (0, j))] * parts
                + [pl.BlockSpec(memory_space=pltpu.SMEM)],
                scratch_shapes=[pltpu.VMEM((slots, 2 * rows), BF16)] * 2
                + [pltpu.VMEM((2 * rows, parts * GROUP), BF16)] * NEAR_GROUPS,
            ),
            out_shape=[jax.ShapeDtypeStruct((slots, LAGS), F32)]
            + [jax.ShapeDtypeStruct((rows, bins), BF16)] * parts
            + [jax.ShapeDtypeStruct((2,), jnp.int32)],
            name="near_pairs",
            **params(60),
        )(
            facts,
            *[flat] * parts,
            *[partner_rows] * parts,
            common,
            table,
            mean,
            *lists,
            common,
            cross_count,
        )

    near_acc, *white, exceeds = near_call()


    def far_call(first, arrays, before):
        pieces = half // piece // 2
        base = 0 if first else pieces
        choose = (lambda s, k: s[7] == k) if first else (lambda s, k: True)
        back_rows = () if first else (BACK_ROWS, slots - BACK_ROWS)
        return pl.pallas_call(
            functools.partial(far_kernel, parts, first),
            grid_spec=pltpu.PrefetchScalarGridSpec(
                num_scalar_prefetch=2,
                grid=(pieces,),
                in_specs=[
                    pl.BlockSpec((rows, piece), lambda j, s, n: (0, base + j)) for _ in range(parts)
                ]
                + [
                    pl.BlockSpec(
                        (rows, piece),
                        functools.partial(
                            lambda k, p, j, s, n: (0, jnp.where(choose(s, k), p * pieces + j, 0)),
                            k,
                            p,
                        ),
                    )
                    for k in range(len(arrays))
                    for p in range(parts)
                ]
                + [
                    pl.BlockSpec((windows, 2, piece), lambda j, s, n: (0, 0, s[6] + base + j)),
                    pl.BlockSpec((2, piece, LAGS), lambda j, s, n: (0, s[6] + base + j, 0)),
                    whole((GROUP, GROUP)),
                    whole((2 * slots, 2 * rows)),
                    whole((2 * slots, 2 * rows)),
                    pl.BlockSpec(memory_space=pl.ANY),
                ],
                out_specs=[pl.BlockSpec(memory_space=pl.ANY)]
                + [whole((n, LAGS)) for n in back_rows],
                scratch_shapes=[
                    pltpu.VMEM((2 * slots, LAGS), F32),
                    pltpu.SemaphoreType.DMA((2 * slots // FAR_BLOCK,)),
                    pltpu.SemaphoreType.DMA((2 * slots // FAR_BLOCK,)),
                ]
                + [pltpu.VMEM((2 * rows, parts * GROUP), BF16)] * (piece // GROUP),
            ),
            out_shape=[jax.ShapeDtypeStruct((2 * slots, LAGS), F32)]
            + [jax.ShapeDtypeStruct((n, LAGS), BF16) for n in back_rows],
            name="far_pairs",
            **params(),
        )(
            facts,
            cross_count,
            *white,
            *[a for a in arrays for _ in range(parts)],
            common,
            table,
            mean,
            hot_a,
            hot_b,
            before,
        )

    (before,) = far_call(True, (far_direct, far_across), near_acc)
    far_acc, theirs, their_rest = far_call(False, (far_second,), before)

    scale = 1.0 / math.sqrt(bins * windows)
    back = lax.ppermute(theirs, "row", slow)
    gathered = pl.pallas_call(
        functools.partial(gather_kernel, scale),
        grid_spec=pltpu.PrefetchScalarGridSpec(
            num_scalar_prefetch=1,
            grid=(1,),
            in_specs=[
                whole((slots, LAGS)),
                whole((slots, 2 * slots)),
                pl.BlockSpec(memory_space=pl.ANY),
            ],
            out_specs=whole((slots, LAGS)),
            scratch_shapes=[
                pltpu.VMEM((2 * slots, LAGS), F32),
                pltpu.SemaphoreType.DMA((2 * slots // FAR_BLOCK,)),
            ],
        ),
        out_shape=jax.ShapeDtypeStruct((slots, LAGS), F32),
        name="gather",
        **params(),
    )(cross_count, near_acc, spread, far_acc)

    def merge(*spread_back):
        return pl.pallas_call(
            functools.partial(merge_kernel, scale),
            grid=(tiles,),
            in_specs=[pl.BlockSpec((tile, LAGS), lambda i: (i, 0))]
            + [
                spec
                for k in range(0, len(spread_back), 2)
                for spec in (
                    pl.BlockSpec((tile, spread_back[k].shape[1]), lambda i: (i, 0)),
                    whole(spread_back[k + 1].shape),
                )
            ],
            out_specs=pl.BlockSpec((tile, LAGS), lambda i: (i, 0)),
            out_shape=jax.ShapeDtypeStruct((slots, LAGS), F32),
            name="merge",
            **params(),
        )(gathered, *spread_back)

    result = lax.cond(
        exceeds[0] > 0,
        lambda: merge(back_spread, back, rest_spread, lax.ppermute(their_rest, "row", slow)),
        lambda: merge(back_spread, back),
    )
    return result.reshape(pair_live.shape + (LAGS,))


def solution(mesh):
    placed = (P(("day", "row"), None, None, None), P("row", None, None), P("row", None))
    return jax.shard_map(
        body, mesh=mesh, in_specs=placed, out_specs=P(("day", "row"), None, None), check_vma=False
    )
```
